256 devices in a mesh: shot: 4 (over x_hi, core), gy: 64 (over z, x_lo, y).
Axes of the slice: x: 4 (x_hi: 2, x_lo: 2; x = x_hi * 2 + x_lo), y: 4, z: 8, core: 2. Of those that a mesh axis runs over, the one named last changes fastest.
Arguments:
- stiffness: float32 [16, 512, 1024], P(None, 'gy'), may hold values from 0.5 to 2
- first_moment: float32 [16, 512, 1024], P('shot', 'gy'), may hold values from -6 to 6
- second_moment: float32 [16, 512, 1024], P('shot', 'gy'), may hold values from 0.1 to 4
- wave_prev: float32 [4, 16, 512, 1024], P('shot', None, 'gy'), may hold values from -6 to 6
- wave_now: float32 [4, 16, 512, 1024], P('shot', None, 'gy'), may hold values from -6 to 6
- adjoint_next: float32 [4, 16, 512, 1024], P('shot', None, 'gy'), may hold values from -6 to 6
- adjoint_now: float32 [4, 16, 512, 1024], P('shot', None, 'gy'), may hold values from -6 to 6
- observed: float32 [4, 4, 512, 128], P('shot', None, 'gy'), may hold values from -12 to 12
- receiver_x: int32 [4, 512, 128], P('shot', 'gy'), may hold values from 0 to 1023
- source_pos: int32 [4, 3], P('shot'), may hold values from 0 to 1023, as said below
- source_wave: float32 [4, 4], P('shot'), may hold values from -240 to 240
Outputs:
- stiffness_new: float32 [16, 512, 1024], P(None, 'gy')
- first_new: float32 [16, 512, 1024], P('shot', 'gy')
- second_new: float32 [16, 512, 1024], P('shot', 'gy')
The draws below stay inside these ranges and needn't reach their ends.
Inputs may be any that keep to these rules, and one draw needn't show every extreme that they name: `source_pos`: each row gives a source cell inside the grid: z below 16, y below 512, x below 1024; some shot's source lies in the last x cell and some shot's in the last y row.
All inputs are finite; a program needn't handle non-finite values.
Results may differ from the reference program's by a relative error of at most 0.00002.
Values sent between devices are 32-bit elements; how exact they have to be, the bound alone decides.
No kernel may reach another device: no remote copies, remote signals or barrier semaphores. Data moves between devices by JAX's collectives and lax.ppermute only.
A program may use at most 128 MiB of HBM per device.

```python
import math
import jax
import jax.numpy as jnp
from jax import lax

NZ = 16
NX = 1024
STEPS = 4
RPR = 128
NY = 512
SHOTS = 4


def draw_source_pos(key, part):
    key = jax.random.fold_in(key, 5)
    first_key, second_key, third_key = jax.random.split(key, 3)
    depth = jax.random.randint(first_key, (SHOTS, 1), 0, NZ)
    across = jax.random.randint(second_key, (SHOTS, 1), 0, NY)
    along = jax.random.randint(third_key, (SHOTS, 1), 0, NX)
    shot_ids = lax.broadcasted_iota(jnp.int32, (SHOTS, 1), 0)
    along = jnp.where(shot_ids == 0, NX - 1, along)
    across = jnp.where(shot_ids == 1, NY - 1, across)
    return jnp.concatenate([depth, across, along], 1).astype(jnp.int32)


def touch_ends(drawn, key, least, top_value):
    longest = drawn.shape.index(max(drawn.shape))
    spots = []
    for shift in (0, 1):
        where = [jax.random.randint(jax.random.fold_in(key, axis), (), 0, length) for axis, length in enumerate(drawn.shape)]
        where[longest] = (where[longest] + shift) % drawn.shape[longest]
        spots.append(tuple(where))
    return drawn.at[spots[0]].set(least).at[spots[1]].set(top_value)


def block_levels(key, extent, cuts, least, top_value):
    gain = 1.0
    for dim, shards_of in cuts:
        steps = jax.random.uniform(jax.random.fold_in(jax.random.fold_in(key, 6), dim), (shards_of,), jnp.float32, least / len(cuts), top_value / len(cuts))
        gain = gain * jnp.repeat(jnp.exp(steps), extent[dim] // shards_of).reshape((-1,) + (1,) * (len(extent) - 1 - dim))
    return gain


def noise(rng, extent, spread, bound, cuts=(), kind=jnp.bfloat16):
    result = jax.random.normal(rng, extent, jnp.float32) * spread
    if len(cuts) > 0:
        result = block_levels(rng, extent, cuts, -0.22, 0.18) * result
    return jnp.clip(result, min=-bound, max=bound).astype(kind)


def setup_inputs(seed: int = 0) -> dict:
    key_of = jax.random.split(jax.random.key(seed), 12)
    return {
        "stiffness": jnp.clip(jnp.exp(math.log(2.0) - 1.3862944 * jax.random.uniform(key_of[0], (NZ, NY, NX), jnp.float32) ** block_levels(key_of[0], (NZ, NY, NX), ((1, 64),), -0.2, 0.2)), 0.5, 2.0),
        "first_moment": noise(key_of[1], (NZ, NY, NX), 1.0, 6.0, ((0, 4), (1, 64)), jnp.float32),
        "second_moment": jnp.clip(jnp.exp(math.log(4.0) - 3.6888794 * jax.random.uniform(key_of[2], (NZ, NY, NX), jnp.float32) ** block_levels(key_of[2], (NZ, NY, NX), ((0, 4), (1, 64)), -0.2, 0.2)), 0.1, 4.0),
        "wave_prev": noise(key_of[3], (SHOTS, NZ, NY, NX), 1.0, 6.0, ((0, 4), (2, 64)), jnp.float32),
        "wave_now": noise(key_of[4], (SHOTS, NZ, NY, NX), 1.0, 6.0, ((0, 4), (2, 64)), jnp.float32),
        "adjoint_next": noise(key_of[5], (SHOTS, NZ, NY, NX), 1.0, 6.0, ((0, 4), (2, 64)), jnp.float32),
        "adjoint_now": noise(key_of[6], (SHOTS, NZ, NY, NX), 1.0, 6.0, ((0, 4), (2, 64)), jnp.float32),
        "observed": noise(key_of[7], (SHOTS, STEPS, NY, RPR), 2.0, 12.0, ((0, 4), (2, 64)), jnp.float32),
        "receiver_x": touch_ends(jax.random.randint(key_of[8], (SHOTS, NY, RPR), 0, NX), jax.random.fold_in(key_of[8], 1), 0, NX - 1).astype(jnp.int32),
        "source_pos": draw_source_pos(jax.random.fold_in(key_of[11], 71), 0),
        "source_wave": noise(key_of[10], (SHOTS, STEPS), 40.0, 240.0, ((0, 4),), jnp.float32),
    }


TIME_STEP_SQ = 0.15
BETA_ONE = 0.9
BETA_TWO = 0.999
LEARN_RATE = 0.05
ADAM_EPS = 1e-08
ADAM_TICKS = 10.0

def toward_next(field, dim_index):
    length = field.shape[dim_index]
    inner = lax.slice_in_dim(field, 1, length, axis=dim_index)
    blank_rows = jnp.zeros_like(lax.slice_in_dim(field, 0, 1, axis=dim_index))
    return jnp.concatenate([inner, blank_rows], dim_index)

def toward_prev(field, dim_index):
    length = field.shape[dim_index]
    inner = lax.slice_in_dim(field, 0, length - 1, axis=dim_index)
    blank_rows = jnp.zeros_like(lax.slice_in_dim(field, 0, 1, axis=dim_index))
    return jnp.concatenate([blank_rows, inner], dim_index)

def operate(field, stiffness):
    summed = jnp.zeros_like(field)
    for dim_index in range(3):
        field_after = toward_next(field, dim_index)
        field_before = toward_prev(field, dim_index)
        stiff_after = toward_next(stiffness, dim_index)
        stiff_before = toward_prev(stiffness, dim_index)
        summed = summed + 0.5 * (stiffness + stiff_after) * (field_after - field) - 0.5 * (stiffness + stiff_before) * (field - field_before)
    return summed

def face_sum(wave, adjoint):
    summed = jnp.zeros_like(wave)
    for dim_index in range(3):
        wave_after = toward_next(wave, dim_index)
        wave_before = toward_prev(wave, dim_index)
        adj_after = toward_next(adjoint, dim_index)
        adj_before = toward_prev(adjoint, dim_index)
        summed = summed + (wave_after - wave) * (adj_after - adjoint) + (wave - wave_before) * (adjoint - adj_before)
    return summed

def one_shot(stiffness, wave_prev, wave_now, adjoint_next, adjoint_now, observed, receiver_x, source_pos, source_wave):
    shape = stiffness.shape
    z_index = lax.broadcasted_iota(jnp.int32, shape, 0)
    y_index = lax.broadcasted_iota(jnp.int32, shape, 1)
    x_index = lax.broadcasted_iota(jnp.int32, shape, 2)
    source_mask = ((z_index == source_pos[0]) & (y_index == source_pos[1]) & (x_index == source_pos[2])).astype(jnp.float32)
    row_ids = jnp.broadcast_to(jnp.arange(NY, dtype=jnp.int32)[:, None], receiver_x.shape)
    waves = [wave_prev, wave_now]
    for level in range(1, STEPS + 1):
        fresh = 2.0 * waves[level] - waves[level - 1] + TIME_STEP_SQ * (operate(waves[level], stiffness) + source_wave[level - 1] * source_mask)
        waves.append(fresh)
    lam_after = adjoint_next
    lam_here = adjoint_now
    gradient = jnp.zeros_like(stiffness)
    for level in range(STEPS + 2, 1, -1):
        gradient = gradient + face_sum(waves[level - 1], lam_here)
        if level >= 3:
            record = jnp.take_along_axis(waves[level - 1][0], receiver_x, axis=1)
            misfit = record - observed[level - 3]
            surface = jnp.zeros((NY, NX), jnp.float32).at[row_ids, receiver_x].add(misfit)
            injected = jnp.concatenate([surface[None], jnp.zeros((NZ - 1, NY, NX), jnp.float32)], 0)
            lam_before = 2.0 * lam_here - lam_after + TIME_STEP_SQ * operate(lam_here, stiffness) + injected
            lam_after = lam_here
            lam_here = lam_before
    return -0.5 * TIME_STEP_SQ * gradient

def reference(stiffness, first_moment, second_moment, wave_prev, wave_now, adjoint_next, adjoint_now, observed, receiver_x, source_pos, source_wave):
    gradient = jnp.zeros_like(stiffness)
    for shot_index in range(SHOTS):
        gradient = gradient + one_shot(stiffness, wave_prev[shot_index], wave_now[shot_index], adjoint_next[shot_index], adjoint_now[shot_index], observed[shot_index], receiver_x[shot_index], source_pos[shot_index], source_wave[shot_index])
    first_new = BETA_ONE * first_moment + (1.0 - BETA_ONE) * gradient
    second_new = BETA_TWO * second_moment + (1.0 - BETA_TWO) * gradient * gradient
    stiffness_new = stiffness - LEARN_RATE * (first_new / (1.0 - BETA_ONE ** ADAM_TICKS)) / (jnp.sqrt(second_new / (1.0 - BETA_TWO ** ADAM_TICKS)) + ADAM_EPS)
    return (stiffness_new, first_new, second_new)
```

```python
import functools

import jax
import jax.numpy as jnp
from jax import lax
from jax.experimental import pallas as pl
from jax.experimental.pallas import tpu as pltpu
from jax.sharding import PartitionSpec as P

TIME_STEP_SQ = 0.15
BETA_ONE = 0.9
BETA_TWO = 0.999
LEARN_RATE = 0.05
ADAM_EPS = 1e-08
ADAM_TICKS = 10.0

NZ = 16
ROWS = 8
XT = 8
LANES = 128
STEPS = 4
REACH = STEPS + 1
EXT = ROWS + 2 * REACH
SIDE_A = 3 * REACH - 1
SIDE_B = 2 * REACH - 1
SURF = STEPS * (STEPS + 1) // 2
HALF = 0.5 * TIME_STEP_SQ

f32 = jnp.float32
VMEM = pl.BlockSpec(memory_space=pltpu.VMEM)
SMEM = pl.BlockSpec(memory_space=pltpu.SMEM)


def native(block):
    planes = block.shape[0]
    return block.reshape(planes, ROWS, XT, LANES).transpose(0, 2, 1, 3).reshape(planes, XT * ROWS, LANES)


def from_native(block):
    planes = block.shape[0]
    return block.reshape(planes, XT, ROWS, LANES).transpose(0, 2, 1, 3).reshape(planes, ROWS, XT * LANES)


def row_of(ref, z, y):
    return ref[z, pl.ds(y, XT, stride=ROWS), :]


def x_next(f, lane):
    r = pltpu.roll(f, LANES - 1, 1)
    return jnp.where(lane == LANES - 1, pltpu.roll(r, XT - 1, 0), r)


def x_prev(f, lane):
    r = pltpu.roll(f, 1, 1)
    return jnp.where(lane == 0, pltpu.roll(r, 1, 0), r)


def iotas():
    lane = lax.broadcasted_iota(jnp.int32, (XT, LANES), 1)
    tile = lax.broadcasted_iota(jnp.int32, (XT, LANES), 0)
    return lane, tile


def pack_kernel(widths, *refs):
    fields, (low, high) = refs[: len(widths)], refs[len(widths) :]

    def plane(z, carry):
        at = 0
        for ref, width in zip(fields, widths, strict=True):
            for k in range(width):
                low[at + k, z] = row_of(ref, z, k)
                high[at + k, z] = row_of(ref, z, ROWS - width + k)
            at += width
        return carry

    lax.fori_loop(0, NZ, plane, 0)


def pack(fields, widths):
    rows = sum(widths)
    shape = jax.ShapeDtypeStruct((rows, NZ, XT, LANES), f32)
    return pl.pallas_call(
        functools.partial(pack_kernel, widths),
        out_shape=(shape, shape),
        in_specs=[VMEM] * len(fields),
        out_specs=(VMEM, VMEM),
        cost_estimate=pl.CostEstimate(flops=0, bytes_accessed=1 << 21, transcendentals=0),
    )(*fields)


def fill(ext, own, low, high, at, width):
    def plane(z, carry):
        for k in range(ROWS):
            ext[REACH + k, z] = row_of(own, z, k)
        return carry

    lax.fori_loop(0, NZ, plane, 0)
    ext[REACH - width : REACH] = low[at : at + width]
    ext[REACH + ROWS : REACH + ROWS + width] = high[at : at + width]


def coefficients(stiff, diag, cx, cy, cz, first, last, lane, tile):
    x_end = (lane == LANES - 1) & (tile == XT - 1)
    x_side = x_end | ((lane == 0) & (tile == 0))

    def rows_y(e, carry):
        for z in range(NZ):
            cy[e, z] = HALF * (stiff[e, z] + stiff[e + 1, z])
        return carry

    lax.fori_loop(0, EXT - 1, rows_y, 0)

    def rows(e, carry):
        below = None
        for z in range(NZ):
            s = stiff[e, z]
            face = jnp.where(x_end, 0.0, HALF * (s + x_next(s, lane)))
            total = face + x_prev(face, lane) + jnp.where(x_side, HALF * s, 0.0)
            above = HALF * (s + stiff[e, z + 1]) if z < NZ - 1 else HALF * s
            total = total + above + (below if z > 0 else HALF * s) + cy[e, z] + cy[e - 1, z]
            cx[e, z] = face
            cz[e, z] = above
            diag[e, z] = 2.0 - total
            below = above
        return carry

    lax.fori_loop(1, EXT - 1, rows, 0)

    @pl.when(first)
    def _():
        cy[REACH - 1] = jnp.zeros((NZ, XT, LANES), f32)

    @pl.when(last)
    def _():
        cy[REACH + ROWS - 1] = jnp.zeros((NZ, XT, LANES), f32)


def leap(now, before, after, diag, cx, cy, cz, lo, hi, lane):
    def rows(e, carry):
        for z in range(NZ):
            u = now[e, z]
            c = cx[e, z]
            acc = diag[e, z] * u - before[e, z]
            acc = acc + c * x_next(u, lane) + x_prev(c * u, lane)
            acc = acc + cy[e, z] * now[e + 1, z] + cy[e - 1, z] * now[e - 1, z]
            if z < NZ - 1:
                acc = acc + cz[e, z] * now[e, z + 1]
            if z > 0:
                acc = acc + cz[e, z - 1] * now[e, z - 1]
            after[e, z] = acc
        return carry

    lax.fori_loop(lo, hi, rows, 0)


def forward_kernel(
    place, source_pos, source_wave, u0, u1, s, low, high, receivers, observed,
    waves, diag, cx, cy, cz, surf, surf_low, surf_high,
    stiff, before,
):
    lane, tile = iotas()
    fill(stiff, s, low, high, 0, REACH)
    fill(waves.at[0], u1, low, high, REACH, REACH)
    fill(before, u0, low, high, 2 * REACH, REACH - 1)
    coefficients(stiff, diag, cx, cy, cz, place[1] == 1, place[2] == 1, lane, tile)
    z_src = source_pos[0, 0]
    e_src = source_pos[0, 1] - place[0] + REACH
    x_src = source_pos[0, 2]
    spot = (tile * LANES + lane) == x_src
    for k in range(STEPS):
        older = before if k == 0 else waves.at[k - 1]
        leap(waves.at[k], older, waves.at[k + 1], diag, cx, cy, cz, k + 1, EXT - 1 - k, lane)

        @pl.when((e_src >= k + 1) & (e_src < EXT - 1 - k))
        def _():
            add = jnp.where(spot, TIME_STEP_SQ * source_wave[0, k], 0.0)
            waves[k + 1, e_src, z_src] = waves[k + 1, e_src, z_src] + add

    column = lax.broadcasted_iota(jnp.int32, (LANES, LANES), 0)
    for y in range(ROWS):
        at = receivers[y : y + 1, :]
        pick = jnp.where(column == (at & (LANES - 1)), 1.0, 0.0)
        held = jnp.where(tile == (at >> 7), 1.0, 0.0)
        top = jnp.concatenate([waves[k, REACH + y, 0] for k in range(1, STEPS + 1)], 0)
        lanes_of = jnp.dot(top, pick, precision=lax.Precision.HIGHEST, preferred_element_type=f32)
        parts = []
        for k in range(STEPS):
            record = jnp.sum(lanes_of[k * XT : (k + 1) * XT] * held, axis=0, keepdims=True)
            parts.append(held * (record - observed[k, y : y + 1, :]))
        back = lax.dot_general(
            jnp.concatenate(parts, 0), pick, (((1,), (1,)), ((), ())),
            precision=lax.Precision.HIGHEST, preferred_element_type=f32,
        )
        for k in range(STEPS):
            surf[k, y] = back[k * XT : (k + 1) * XT]
    at = 0
    for k in range(STEPS - 1, -1, -1):
        width = k + 1
        surf_low[at : at + width] = surf[k, :width]
        surf_high[at : at + width] = surf[k, ROWS - width :]
        at += width


def forward(place, source_pos, source_wave, u0, u1, s, low, high, receivers, observed):
    field = (EXT, NZ, XT, LANES)
    one = jax.ShapeDtypeStruct(field, f32)
    edge = jax.ShapeDtypeStruct((SURF, XT, LANES), f32)
    return pl.pallas_call(
        forward_kernel,
        out_shape=(
            jax.ShapeDtypeStruct((STEPS + 1, *field), f32),
            one, one, one, one,
            jax.ShapeDtypeStruct((STEPS, ROWS, XT, LANES), f32),
            edge, edge,
        ),
        in_specs=[SMEM] * 3 + [VMEM] * 7,
        out_specs=(VMEM,) * 8,
        scratch_shapes=[pltpu.VMEM(field, f32)] * 2,
        compiler_params=pltpu.CompilerParams(vmem_limit_bytes=40 << 20),
        cost_estimate=pl.CostEstimate(flops=1 << 25, bytes_accessed=1 << 24, transcendentals=0),
    )(place, source_pos, source_wave, u0, u1, s, low, high, receivers, observed)


def adjoint_kernel(
    place, l6, l7, low, high, waves, diag, cx, cy, cz, surf, surf_low, surf_high,
    keep, send,
    lams, before, face_y, grad,
):
    lane, tile = iotas()
    x_end = (lane == LANES - 1) & (tile == XT - 1)
    x_side = x_end | ((lane == 0) & (tile == 0))
    fill(lams.at[0], l6, low, high, 0, REACH)
    fill(before, l7, low, high, REACH, REACH - 1)
    at = 0
    for k in range(STEPS):
        older = before if k == 0 else lams.at[k - 1]
        leap(lams.at[k], older, lams.at[k + 1], diag, cx, cy, cz, k + 1, EXT - 1 - k, lane)
        width = STEPS - k
        for j in range(width):
            e = REACH - width + j
            lams[k + 1, e, 0] = lams[k + 1, e, 0] + surf_low[at + j]
            e = REACH + ROWS + j
            lams[k + 1, e, 0] = lams[k + 1, e, 0] + surf_high[at + j]
        for j in range(ROWS):
            e = REACH + j
            lams[k + 1, e, 0] = lams[k + 1, e, 0] + surf[STEPS - 1 - k, j]
        at += width

    levels = STEPS + 1

    def edge_rows(z, carry):
        total = None
        for n in range(levels):
            m = STEPS - n
            part = (waves[n, REACH, z] - waves[n, REACH - 1, z]) * (lams[m, REACH, z] - lams[m, REACH - 1, z])
            total = part if total is None else total + part
        face_y[z] = total
        return carry

    lax.fori_loop(0, NZ, edge_rows, 0)

    def rows(y, carry):
        e = y + REACH
        below = None
        us = [waves[n, e, 0] for n in range(levels)]
        ls = [lams[STEPS - n, e, 0] for n in range(levels)]
        for z in range(NZ):
            fx = fy = fz = cell = None
            next_us, next_ls = [], []
            for n in range(levels):
                m = STEPS - n
                u, l = us[n], ls[n]
                px = (x_next(u, lane) - u) * (x_next(l, lane) - l)
                py = (waves[n, e + 1, z] - u) * (lams[m, e + 1, z] - l)
                both = u * l
                if z < NZ - 1:
                    un, ln = waves[n, e, z + 1], lams[m, e, z + 1]
                    next_us.append(un)
                    next_ls.append(ln)
                    pz = (un - u) * (ln - l)
                else:
                    pz = both
                fx = px if fx is None else fx + px
                fy = py if fy is None else fy + py
                fz = pz if fz is None else fz + pz
                cell = both if cell is None else cell + both
            us, ls = next_us, next_ls
            fx = jnp.where(x_end, 0.0, fx)
            total = fx + x_prev(fx, lane) + jnp.where(x_side, cell, 0.0)
            total = total + fy + face_y[z] + fz + (cell if z == 0 else below)
            face_y[z] = fy
            below = fz
            grad[z, pl.ds(y, XT, stride=ROWS), :] = -HALF * total
        return carry

    lax.fori_loop(0, ROWS, rows, 0)
    core = place[3]
    for group in range(2):
        keep[group] = grad[pl.ds(8 * group + 4 * core, 4)]
        send[group] = grad[pl.ds(8 * group + 4 * (1 - core), 4)]


def adjoint(place, l6, l7, low, high, waves, diag, cx, cy, cz, surf, surf_low, surf_high):
    field = (EXT, NZ, XT, LANES)
    part = jax.ShapeDtypeStruct((2, 4, XT * ROWS, LANES), f32)
    return pl.pallas_call(
        adjoint_kernel,
        out_shape=(part, part),
        in_specs=[SMEM] + [VMEM] * 12,
        out_specs=(VMEM, VMEM),
        scratch_shapes=[
            pltpu.VMEM((STEPS + 1, *field), f32),
            pltpu.VMEM(field, f32),
            pltpu.VMEM((NZ, XT, LANES), f32),
            pltpu.VMEM((NZ, XT * ROWS, LANES), f32),
        ],
        compiler_params=pltpu.CompilerParams(vmem_limit_bytes=40 << 20),
        cost_estimate=pl.CostEstimate(flops=1 << 25, bytes_accessed=1 << 24, transcendentals=0),
    )(place, l6, l7, low, high, waves, diag, cx, cy, cz, surf, surf_low, surf_high)


def to_next(block):
    count = lax.axis_size("gy")
    return lax.ppermute(block, "gy", [(i, i + 1) for i in range(count - 1)])


def to_prev(block):
    count = lax.axis_size("gy")
    return lax.ppermute(block, "gy", [(i + 1, i) for i in range(count - 1)])


def swap_core(block):
    return lax.ppermute(block, "shot", [(0, 1), (1, 0), (2, 3), (3, 2)])


def swap_far(block):
    return lax.ppermute(block, "shot", [(0, 2), (2, 0), (1, 3), (3, 1)])


def body(
    stiffness,
    first_moment,
    second_moment,
    wave_prev,
    wave_now,
    adjoint_next,
    adjoint_now,
    observed,
    receiver_x,
    source_pos,
    source_wave,
):
    gy = lax.axis_index("gy")
    shot = lax.axis_index("shot")
    core, far = shot % 2, shot // 2
    place = jnp.stack([gy * ROWS, gy == 0, gy == lax.axis_size("gy") - 1, core]).astype(jnp.int32)
    s = native(stiffness)
    u0, u1 = native(wave_prev[0]), native(wave_now[0])
    l6, l7 = native(adjoint_now[0]), native(adjoint_next[0])
    first, second = native(first_moment), native(second_moment)

    a_low, a_high = pack((s, u1, u0), (REACH, REACH, REACH - 1))
    a_high, a_low = to_next(a_high), to_prev(a_low)
    b_low, b_high = pack((l6, l7), (REACH, REACH - 1))
    b_high, b_low = to_next(b_high), to_prev(b_low)
    moments = swap_far(jnp.stack([first, second]))

    waves, diag, cx, cy, cz, surf, surf_low, surf_high = forward(
        place, source_pos, source_wave, u0, u1, s, a_high, a_low, receiver_x[0], observed[0]
    )
    surf_high, surf_low = to_next(surf_high), to_prev(surf_low)
    keep, send = adjoint(
        place, l6, l7, b_high, b_low, waves, diag, cx, cy, cz, surf, surf_high, surf_low
    )
    chip_sum = keep + swap_core(send)
    share = chip_sum + swap_far(chip_sum)

    is_far = (jnp.arange(2) == far)[:, None, None, None]
    first_two = jnp.where(is_far, first[None], moments[0][None])
    second_two = jnp.where(is_far, second[None], moments[1][None])
    stiff_two = jnp.where(core == 0, s.reshape(2, 2, 4, XT * ROWS, LANES)[:, 0], s.reshape(2, 2, 4, XT * ROWS, LANES)[:, 1])
    first_new = BETA_ONE * first_two + (1.0 - BETA_ONE) * share
    second_new = BETA_TWO * second_two + (1.0 - BETA_TWO) * share * share
    updated = stiff_two - LEARN_RATE * (first_new / (1.0 - BETA_ONE**ADAM_TICKS)) / (
        jnp.sqrt(second_new / (1.0 - BETA_TWO**ADAM_TICKS)) + ADAM_EPS
    )
    other = swap_core(updated)
    even = jnp.where(core == 0, updated, other)
    odd = jnp.where(core == 0, other, updated)
    stiffness_new = jnp.stack([even, odd], 1).reshape(NZ, XT * ROWS, LANES)
    first_out = jnp.where(far == 0, first_new[0], first_new[1])
    second_out = jnp.where(far == 0, second_new[0], second_new[1])
    return (from_native(stiffness_new), from_native(first_out), from_native(second_out))


def solution(mesh):
    return jax.shard_map(
        body,
        mesh=mesh,
        in_specs=(
            P(None, "gy", None),
            P("shot", "gy", None),
            P("shot", "gy", None),
            P("shot", None, "gy", None),
            P("shot", None, "gy", None),
            P("shot", None, "gy", None),
            P("shot", None, "gy", None),
            P("shot", None, "gy", None),
            P("shot", "gy", None),
            P("shot", None),
            P("shot", None),
        ),
        out_specs=(P(None, "gy", None), P("shot", "gy", None), P("shot", "gy", None)),
        check_vma=False,
    )
```

```python
import functools

import jax
import jax.numpy as jnp
from jax import lax
from jax.experimental import pallas as pl
from jax.experimental.pallas import tpu as pltpu
from jax.sharding import PartitionSpec as P

TIME_STEP_SQ = 0.15
BETA_ONE = 0.9
BETA_TWO = 0.999
LEARN_RATE = 0.05
ADAM_EPS = 1e-08
ADAM_TICKS = 10.0

NZ = 16
ROWS = 8
XT = 8
LANES = 128
STEPS = 4
REACH = STEPS + 1
EDGE = STEPS
CONE = STEPS - 1
OFF = ROWS
EXT = ROWS + 2 * OFF
FIELD = (EXT, NZ, XT, LANES)
SURF_ROWS = ROWS + 2 * EDGE
TILE_A = (3 * REACH - 1) * NZ + CONE * (3 * REACH - 1) + 2
TILE_B = (2 * REACH - 1) * NZ
HALF = 0.5 * TIME_STEP_SQ

f32 = jnp.float32
VMEM = pl.BlockSpec(memory_space=pltpu.VMEM)
SMEM = pl.BlockSpec(memory_space=pltpu.SMEM)


def native(block):
    planes = block.shape[0]
    return block.reshape(planes, ROWS, XT, LANES).transpose(0, 2, 1, 3).reshape(planes, XT * ROWS, LANES)


def from_native(block):
    planes = block.shape[0]
    return block.reshape(planes, XT, ROWS, LANES).transpose(0, 2, 1, 3).reshape(planes, ROWS, XT * LANES)


def row_of(ref, z, y):
    return ref[z, pl.ds(y, XT, stride=ROWS), :]


def x_next(f, lane):
    r = pltpu.roll(f, LANES - 1, 1)
    return jnp.where(lane == LANES - 1, pltpu.roll(r, XT - 1, 0), r)


def x_prev(f, lane):
    r = pltpu.roll(f, 1, 1)
    return jnp.where(lane == 0, pltpu.roll(r, 1, 0), r)


def iotas():
    lane = lax.broadcasted_iota(jnp.int32, (XT, LANES), 1)
    tile = lax.broadcasted_iota(jnp.int32, (XT, LANES), 0)
    return lane, tile


def in_blocks(lo, hi, size, rows):
    whole = (hi - lo) // size
    if whole:
        lax.fori_loop(0, whole, lambda i, c: (rows(lo + i * size, size), c)[1], 0)
    if (hi - lo) % size:
        rows(lo + whole * size, (hi - lo) % size)


def pack_fields(fields, widths, low, high, at):
    def plane(z, carry):
        first = at
        for ref, width in zip(fields, widths, strict=True):
            for k in range(width):
                low[first + k * NZ + z] = row_of(ref, z, k)
                high[first + k * NZ + z] = row_of(ref, z, ROWS - width + k)
            first += width * NZ
        return carry

    lax.fori_loop(0, NZ, plane, 0)
    return at + sum(widths) * NZ


def pack_first_kernel(s, u1, u0, receivers, observed, low, high):
    widths = (REACH, REACH, REACH - 1)
    at = pack_fields((s, u1, u0), widths, low, high, 0)
    for ref, width in zip((s, u1, u0), widths, strict=True):
        for k in range(CONE):
            for z in range(width):
                low[at + z] = row_of(ref, z, width + k)
                high[at + z] = row_of(ref, z, ROWS - width - CONE + k)
            at += width
    where = receivers[...].astype(f32)
    empty = jnp.zeros((2, LANES), f32)
    for side, rows in ((low, lambda n: slice(0, n)), (high, lambda n: slice(ROWS - n, ROWS))):
        parts = [where[rows(EDGE)]]
        for k in range(STEPS - 1, -1, -1):
            parts.append(observed[k][rows(k + 1)])
        parts.append(empty)
        both = jnp.concatenate(parts, 0)
        side[at] = both[:XT]
        side[at + 1] = both[XT:]


def pack_first(s, u1, u0, receivers, observed):
    shape = jax.ShapeDtypeStruct((TILE_A, XT, LANES), f32)
    return pl.pallas_call(
        pack_first_kernel,
        out_shape=(shape, shape),
        in_specs=[VMEM] * 5,
        out_specs=(VMEM, VMEM),
        cost_estimate=pl.CostEstimate(flops=0, bytes_accessed=1 << 21, transcendentals=0),
        name="pack_first",
    )(s, u1, u0, receivers, observed)


def pack_second_kernel(l6, l7, low, high):
    pack_fields((l6, l7), (REACH, REACH - 1), low, high, 0)


def pack_second(l6, l7):
    shape = jax.ShapeDtypeStruct((TILE_B, XT, LANES), f32)
    return pl.pallas_call(
        pack_second_kernel,
        out_shape=(shape, shape),
        in_specs=[VMEM] * 2,
        out_specs=(VMEM, VMEM),
        cost_estimate=pl.CostEstimate(flops=0, bytes_accessed=1 << 21, transcendentals=0),
        name="pack_second",
    )(l6, l7)


def fill(ext, own, low, high, at, width):
    def plane(z, carry):
        for k in range(ROWS):
            ext[OFF + k, z] = row_of(own, z, k)
        return carry

    lax.fori_loop(0, NZ, plane, 0)
    for k in range(width):
        ext[OFF - width + k] = low[at + k * NZ : at + (k + 1) * NZ]
        ext[OFF + ROWS + k] = high[at + k * NZ : at + (k + 1) * NZ]


def fill_cone(ext, low, high, at, width):
    for k in range(CONE):
        ext[OFF - width - CONE + k, :width] = low[at + k * width : at + (k + 1) * width]
        ext[OFF + ROWS + width + k, :width] = high[at + k * width : at + (k + 1) * width]


def coefficients(stiff, diag, cx, cy, cz, lo, hi, planes, lane, tile):
    x_end = (lane == LANES - 1) & (tile == XT - 1)
    x_start = (lane == 0) & (tile == 0)

    def faces(first, count):
        for e in (first + r for r in range(count)):
            for z in range(planes):
                cy[e, z] = HALF * (stiff[e, z] + stiff[e + 1, z])

    def rows(first, count):
        for e in (first + r for r in range(count)):
            below = None
            following = HALF * stiff[e, 0]
            for z in range(planes):
                s = following
                face = s + jnp.where(x_end, 0.0, x_next(s, lane))
                total = face + (s + jnp.where(x_start, 0.0, x_prev(s, lane)))
                if z < NZ - 1:
                    following = HALF * stiff[e, z + 1]
                    above = s + following
                else:
                    above = s
                total = total + above + (below if z > 0 else s) + cy[e, z] + cy[e - 1, z]
                cx[e, z] = jnp.where(x_end, 0.0, face)
                cz[e, z] = above
                diag[e, z] = 2.0 - total
                below = above

    in_blocks(lo - 1, hi, 4, faces)
    in_blocks(lo, hi, 4, rows)


def leap(now, before, after, diag, cx, cy, cz, lo, hi, planes, lane):
    def rows(first, count):
        for e in (first + r for r in range(count)):
            for z in range(planes):
                u = now[e, z]
                c = cx[e, z]
                acc = diag[e, z] * u - before[e, z]
                acc = acc + c * x_next(u, lane) + x_prev(c * u, lane)
                acc = acc + cy[e, z] * now[e + 1, z] + cy[e - 1, z] * now[e - 1, z]
                if z < NZ - 1:
                    acc = acc + cz[e, z] * now[e, z + 1]
                if z > 0:
                    acc = acc + cz[e, z - 1] * now[e, z - 1]
                after[e, z] = acc

    in_blocks(lo, hi, 4, rows)


def forward_kernel(
    place, source_pos, source_wave, u0, u1, s, low, high, receivers, observed,
    w1, w2, w3, w4, w5, diag, cx, cy, cz, surf,
    stiff, before,
):
    lane, tile = iotas()
    waves = (w1, w2, w3, w4, w5)
    at = 0
    for ext, own, width in ((stiff, s, REACH), (w1, u1, REACH), (before, u0, REACH - 1)):
        fill(ext, own, low, high, at, width)
        at += width * NZ
    for ext, width in ((stiff, REACH), (w1, REACH), (before, REACH - 1)):
        fill_cone(ext, low, high, at, width)
        at += width * CONE
    top, bottom = OFF - REACH, OFF + ROWS + REACH
    for lo, hi, planes in (
        (top + 1, bottom - 1, NZ),
        (top + 1 - CONE, top + 1, STEPS),
        (bottom - 1, bottom - 1 + CONE, STEPS),
    ):
        coefficients(stiff, diag, cx, cy, cz, lo, hi, planes, lane, tile)

    @pl.when(place[1] == 1)
    def _():
        cy[OFF - 1] = jnp.zeros((NZ, XT, LANES), f32)

    @pl.when(place[2] == 1)
    def _():
        cy[OFF + ROWS - 1] = jnp.zeros((NZ, XT, LANES), f32)

    z_src = source_pos[0, 0]
    e_src = source_pos[0, 1] - place[0] + OFF
    x_src = source_pos[0, 2]
    spot = (tile * LANES + lane) == x_src
    for k in range(STEPS):
        older = before if k == 0 else waves[k - 1]
        after = waves[k + 1]
        lo, hi = top + 1 + k, bottom - 1 - k
        leap(waves[k], older, after, diag, cx, cy, cz, lo, hi, NZ, lane)
        leap(waves[k], older, after, diag, cx, cy, cz, lo - CONE, lo, STEPS - k, lane)
        leap(waves[k], older, after, diag, cx, cy, cz, hi, hi + CONE, STEPS - k, lane)

        @pl.when((e_src >= lo - CONE) & (e_src < hi + CONE))
        def _():
            add = jnp.where(spot, TIME_STEP_SQ * source_wave[0, k], 0.0)
            after[e_src, z_src] = after[e_src, z_src] + add

    column = lax.broadcasted_iota(jnp.int32, (LANES, LANES), 0)
    sides = []
    for ref in (low, high):
        rows = jnp.concatenate([ref[TILE_A - 2], ref[TILE_A - 1]], 0)
        sides.append((rows[:EDGE].astype(jnp.int32), rows[EDGE:]))
    for j in range(SURF_ROWS):
        y = j - EDGE
        if y < 0:
            used = range(-y - 1, STEPS)
            at = sides[0][0][j : j + 1]
        elif y < ROWS:
            used = range(STEPS)
            at = receivers[y : y + 1, :]
        else:
            used = range(y - ROWS, STEPS)
            at = sides[1][0][y - ROWS : y - ROWS + 1]
        pick = jnp.where(column == (at & (LANES - 1)), 1.0, 0.0)
        held = jnp.where(tile == (at >> 7), 1.0, 0.0)
        surface = jnp.concatenate([waves[k + 1][OFF + y, 0] for k in used], 0)
        lanes_of = jnp.dot(surface, pick, precision=lax.Precision.HIGHEST, preferred_element_type=f32)
        parts = []
        for i, k in enumerate(used):
            record = jnp.sum(lanes_of[i * XT : (i + 1) * XT] * held, axis=0, keepdims=True)
            if 0 <= y < ROWS:
                trace = observed[k, y : y + 1, :]
            else:
                skip = sum(m + 1 for m in range(k + 1, STEPS))
                r = skip + (y + k + 1 if y < 0 else y - ROWS)
                trace = sides[0 if y < 0 else 1][1][r : r + 1]
            parts.append(held * (record - trace))
        back = lax.dot_general(
            jnp.concatenate(parts, 0), pick, (((1,), (1,)), ((), ())),
            precision=lax.Precision.HIGHEST, preferred_element_type=f32,
        )
        for i, k in enumerate(used):
            surf[k, j] = back[i * XT : (i + 1) * XT]


def forward(place, source_pos, source_wave, u0, u1, s, low, high, receivers, observed):
    one = jax.ShapeDtypeStruct(FIELD, f32)
    return pl.pallas_call(
        forward_kernel,
        out_shape=(one,) * (STEPS + 5) + (jax.ShapeDtypeStruct((STEPS, SURF_ROWS, XT, LANES), f32),),
        in_specs=[SMEM] * 3 + [VMEM] * 7,
        out_specs=(VMEM,) * (STEPS + 6),
        scratch_shapes=[pltpu.VMEM(FIELD, f32)] * 2,
        compiler_params=pltpu.CompilerParams(vmem_limit_bytes=26 << 20),
        cost_estimate=pl.CostEstimate(flops=1 << 25, bytes_accessed=1 << 24, transcendentals=0),
        name="forward",
    )(place, source_pos, source_wave, u0, u1, s, low, high, receivers, observed)


def adjoint_kernel(
    place, l6, l7, low, high, w1, w2, w3, w4, w5, diag, cx, cy, cz, surf,
    keep, send,
    m6, m5, m4, m3, m2, before, face_y, grad,
):
    lane, tile = iotas()
    x_end = (lane == LANES - 1) & (tile == XT - 1)
    x_side = x_end | ((lane == 0) & (tile == 0))
    lams = (m6, m5, m4, m3, m2)
    fill(m6, l6, low, high, 0, REACH)
    fill(before, l7, low, high, REACH * NZ, REACH - 1)
    for k in range(STEPS):
        older = before if k == 0 else lams[k - 1]
        after = lams[k + 1]
        lo, hi = OFF - REACH + 1 + k, OFF + ROWS + REACH - 1 - k
        leap(lams[k], older, after, diag, cx, cy, cz, lo, hi, NZ, lane)
        for e in range(lo, hi):
            after[e, 0] = after[e, 0] + surf[STEPS - 1 - k, e - OFF + EDGE]

    pairs = tuple(zip((w5, w4, w3, w2, w1), lams, strict=True))
    for z in range(NZ):
        total = None
        for w, m in pairs:
            part = (w[OFF, z] - w[OFF - 1, z]) * (m[OFF, z] - m[OFF - 1, z])
            total = part if total is None else total + part
        face_y[z] = total

    def row(y, carry):
        e = y + OFF
        below = None
        us = [w[e, 0] for w, _ in pairs]
        ls = [m[e, 0] for _, m in pairs]
        for z in range(NZ):
            fx = fy = fz = cell = None
            next_us, next_ls = [], []
            for (w, m), u, l in zip(pairs, us, ls, strict=True):
                px = (x_next(u, lane) - u) * (x_next(l, lane) - l)
                py = (w[e + 1, z] - u) * (m[e + 1, z] - l)
                both = u * l
                if z < NZ - 1:
                    un, ln = w[e, z + 1], m[e, z + 1]
                    next_us.append(un)
                    next_ls.append(ln)
                    pz = (un - u) * (ln - l)
                else:
                    pz = both
                fx = px if fx is None else fx + px
                fy = py if fy is None else fy + py
                fz = pz if fz is None else fz + pz
                cell = both if cell is None else cell + both
            us, ls = next_us, next_ls
            fx = jnp.where(x_end, 0.0, fx)
            total = fx + x_prev(fx, lane) + jnp.where(x_side, cell, 0.0)
            total = total + fy + face_y[z] + fz + (cell if z == 0 else below)
            face_y[z] = fy
            below = fz
            grad[z, pl.ds(y, XT, stride=ROWS), :] = -HALF * total
        return carry

    lax.fori_loop(0, ROWS, row, 0)
    core = place[3]
    for group in range(2):
        keep[group] = grad[pl.ds(8 * group + 4 * core, 4)]
        send[group] = grad[pl.ds(8 * group + 4 * (1 - core), 4)]


def adjoint(place, l6, l7, low, high, *rest):
    part = jax.ShapeDtypeStruct((2, 4, XT * ROWS, LANES), f32)
    return pl.pallas_call(
        adjoint_kernel,
        out_shape=(part, part),
        in_specs=[SMEM] + [VMEM] * (4 + len(rest)),
        out_specs=(VMEM, VMEM),
        scratch_shapes=[pltpu.VMEM(FIELD, f32)] * (STEPS + 2)
        + [
            pltpu.VMEM((NZ, XT, LANES), f32),
            pltpu.VMEM((NZ, XT * ROWS, LANES), f32),
        ],
        compiler_params=pltpu.CompilerParams(vmem_limit_bytes=30 << 20),
        cost_estimate=pl.CostEstimate(flops=1 << 25, bytes_accessed=1 << 24, transcendentals=0),
        name="adjoint",
    )(place, l6, l7, low, high, *rest)


def to_next(block):
    count = lax.axis_size("gy")
    return lax.ppermute(block, "gy", [(i, i + 1) for i in range(count - 1)])


def to_prev(block):
    count = lax.axis_size("gy")
    return lax.ppermute(block, "gy", [(i + 1, i) for i in range(count - 1)])


def swap_core(block):
    return lax.ppermute(block, "shot", [(0, 1), (1, 0), (2, 3), (3, 2)])


def swap_far(block):
    return lax.ppermute(block, "shot", [(0, 2), (2, 0), (1, 3), (3, 1)])


def body(
    stiffness,
    first_moment,
    second_moment,
    wave_prev,
    wave_now,
    adjoint_next,
    adjoint_now,
    observed,
    receiver_x,
    source_pos,
    source_wave,
):
    gy = lax.axis_index("gy")
    shot = lax.axis_index("shot")
    core, far = shot % 2, shot // 2
    place = jnp.stack([gy * ROWS, gy == 0, gy == lax.axis_size("gy") - 1, core]).astype(jnp.int32)
    s = native(stiffness)
    u0, u1 = native(wave_prev[0]), native(wave_now[0])
    l6, l7 = native(adjoint_now[0]), native(adjoint_next[0])
    first, second = native(first_moment), native(second_moment)

    a_low, a_high = pack_first(s, u1, u0, receiver_x[0], observed[0])
    a_high, a_low = to_next(a_high), to_prev(a_low)
    b_low, b_high = pack_second(l6, l7)
    b_high, b_low = to_next(b_high), to_prev(b_low)
    moments = swap_far(jnp.stack([first, second]))
    a_high, a_low, moments = lax.optimization_barrier((a_high, a_low, moments))

    fields = forward(
        place, source_pos, source_wave, u0, u1, s, a_high, a_low, receiver_x[0], observed[0]
    )
    keep, send = adjoint(place, l6, l7, b_high, b_low, *fields)
    chip_sum = keep + swap_core(send)
    share = chip_sum + swap_far(chip_sum)

    is_far = (jnp.arange(2) == far)[:, None, None, None]
    first_two = jnp.where(is_far, first[None], moments[0][None])
    second_two = jnp.where(is_far, second[None], moments[1][None])
    stiff_two = jnp.where(core == 0, s.reshape(2, 2, 4, XT * ROWS, LANES)[:, 0], s.reshape(2, 2, 4, XT * ROWS, LANES)[:, 1])
    first_new = BETA_ONE * first_two + (1.0 - BETA_ONE) * share
    second_new = BETA_TWO * second_two + (1.0 - BETA_TWO) * share * share
    updated = stiff_two - LEARN_RATE * (first_new / (1.0 - BETA_ONE**ADAM_TICKS)) / (
        jnp.sqrt(second_new / (1.0 - BETA_TWO**ADAM_TICKS)) + ADAM_EPS
    )
    other = swap_core(updated)
    even = jnp.where(core == 0, updated, other)
    odd = jnp.where(core == 0, other, updated)
    stiffness_new = jnp.stack([even, odd], 1).reshape(NZ, XT * ROWS, LANES)
    first_out = jnp.where(far == 0, first_new[0], first_new[1])
    second_out = jnp.where(far == 0, second_new[0], second_new[1])
    return (from_native(stiffness_new), from_native(first_out), from_native(second_out))


def solution(mesh):
    return jax.shard_map(
        body,
        mesh=mesh,
        in_specs=(
            P(None, "gy", None),
            P("shot", "gy", None),
            P("shot", "gy", None),
            P("shot", None, "gy", None),
            P("shot", None, "gy", None),
            P("shot", None, "gy", None),
            P("shot", None, "gy", None),
            P("shot", None, "gy", None),
            P("shot", "gy", None),
            P("shot", None),
            P("shot", None),
        ),
        out_specs=(P(None, "gy", None), P("shot", "gy", None), P("shot", "gy", None)),
        check_vma=False,
    )
```

```python
import functools

import jax
import jax.numpy as jnp
from jax import lax
from jax.experimental import pallas as pl
from jax.experimental.pallas import tpu as pltpu
from jax.sharding import PartitionSpec as P

TIME_STEP_SQ = 0.15
BETA_ONE = 0.9
BETA_TWO = 0.999
LEARN_RATE = 0.05
ADAM_EPS = 1e-08
ADAM_TICKS = 10.0

NZ = 16
ROWS = 8
XT = 8
LANES = 128
STEPS = 4
REACH = STEPS + 1
EDGE = STEPS
CONE = STEPS - 1
OFF = ROWS
EXT = ROWS + 2 * OFF
FIELD = (EXT, NZ, XT, LANES)
SHORT = (ROWS + 2 * REACH, NZ, XT, LANES)
SURF_ROWS = ROWS + 2 * EDGE
PART = NZ // 2
TILE_S = REACH * PART + CONE * REACH
TILE_U = (2 * REACH - 1) * (NZ + CONE) + 2
TILE_L = (2 * REACH - 1) * NZ
HALF = 0.5 * TIME_STEP_SQ

f32 = jnp.float32
VMEM = pl.BlockSpec(memory_space=pltpu.VMEM)
SMEM = pl.BlockSpec(memory_space=pltpu.SMEM)


def native(block):
    planes = block.shape[0]
    return block.reshape(planes, ROWS, XT, LANES).transpose(0, 2, 1, 3).reshape(planes, XT * ROWS, LANES)


def from_native(block):
    planes = block.shape[0]
    return block.reshape(planes, XT, ROWS, LANES).transpose(0, 2, 1, 3).reshape(planes, ROWS, XT * LANES)


def row_of(ref, z, y):
    return ref[z, pl.ds(y, XT, stride=ROWS), :]


def x_next(f, lane):
    r = pltpu.roll(f, LANES - 1, 1)
    return jnp.where(lane == LANES - 1, pltpu.roll(r, XT - 1, 0), r)


def x_prev(f, lane):
    r = pltpu.roll(f, 1, 1)
    return jnp.where(lane == 0, pltpu.roll(r, 1, 0), r)


def iotas():
    lane = lax.broadcasted_iota(jnp.int32, (XT, LANES), 1)
    tile = lax.broadcasted_iota(jnp.int32, (XT, LANES), 0)
    return lane, tile


def in_blocks(lo, hi, size, rows):
    whole = (hi - lo) // size
    if whole:
        lax.fori_loop(0, whole, lambda i, c: (rows(lo + i * size, size), c)[1], 0)
    if (hi - lo) % size:
        rows(lo + whole * size, (hi - lo) % size)


def pack_fields(fields, widths, low, high, at):
    def plane(z, carry):
        first = at
        for ref, width in zip(fields, widths, strict=True):
            for k in range(width):
                low[first + k * NZ + z] = row_of(ref, z, k)
                high[first + k * NZ + z] = row_of(ref, z, ROWS - width + k)
            first += width * NZ
        return carry

    lax.fori_loop(0, NZ, plane, 0)
    return at + sum(widths) * NZ


def core_index():
    return lax.rem(lax.axis_index("shot"), 2)


def by_parity(pair, work):
    parity = lax.rem(lax.axis_index("gy"), 2)

    @pl.when(parity == 0)
    def _():
        work(pair[1], pair[0])

    @pl.when(parity == 1)
    def _():
        work(pair[0], pair[1])


def pack_cone(ref, width, low, high, at):
    for k in range(CONE):
        for z in range(width):
            low[at + z] = row_of(ref, z, width + k)
            high[at + z] = row_of(ref, z, ROWS - width - CONE + k)
        at += width
    return at


def pack_stiffness_kernel(s, *pair):
    base = core_index() * PART

    def work(low, high):
        def plane(z, carry):
            for k in range(REACH):
                low[k * PART + z] = row_of(s, base + z, k)
                high[k * PART + z] = row_of(s, base + z, ROWS - REACH + k)
            return carry

        lax.fori_loop(0, PART, plane, 0)
        pack_cone(s, REACH, low, high, REACH * PART)

    by_parity(pair, work)


def pack_waves_kernel(u1, u0, receivers, observed, *pair):
    def work(low, high):
        at = pack_fields((u1, u0), (REACH, REACH - 1), low, high, 0)
        at = pack_cone(u1, REACH, low, high, at)
        at = pack_cone(u0, REACH - 1, low, high, at)
        where = receivers[...].astype(f32)
        empty = jnp.zeros((2, LANES), f32)
        for side, rows in ((low, lambda n: slice(0, n)), (high, lambda n: slice(ROWS - n, ROWS))):
            parts = [where[rows(EDGE)]]
            for k in range(STEPS - 1, -1, -1):
                parts.append(observed[k][rows(k + 1)])
            parts.append(empty)
            both = jnp.concatenate(parts, 0)
            side[at] = both[:XT]
            side[at + 1] = both[XT:]

    by_parity(pair, work)


def pack_adjoint_kernel(l6, l7, *pair):
    by_parity(pair, lambda low, high: pack_fields((l6, l7), (REACH, REACH - 1), low, high, 0))


def pack(kernel, name, tiles, *arrays):
    shape = pltpu.VMEM((tiles, XT, LANES), f32)
    return pl.pallas_call(
        kernel,
        out_shape=(shape, shape),
        in_specs=[VMEM] * len(arrays),
        out_specs=(VMEM, VMEM),
        compiler_params=pltpu.CompilerParams(vmem_limit_bytes=6 << 20),
        cost_estimate=pl.CostEstimate(flops=0, bytes_accessed=1 << 21, transcendentals=0),
        name=name,
    )(*arrays)


def fill(ext, own, off):
    def plane(z, carry):
        for k in range(ROWS):
            ext[off + k, z] = row_of(own, z, k)
        return carry

    lax.fori_loop(0, NZ, plane, 0)


def fill_halo(ext, off, low, high, at, width):
    for k in range(width):
        ext[off - width + k] = low[at + k * NZ : at + (k + 1) * NZ]
        ext[off + ROWS + k] = high[at + k * NZ : at + (k + 1) * NZ]


def fill_cone(ext, low, high, at, width):
    for k in range(CONE):
        ext[OFF - width - CONE + k, :width] = low[at + k * width : at + (k + 1) * width]
        ext[OFF + ROWS + width + k, :width] = high[at + k * width : at + (k + 1) * width]


def coefficients(stiff, diag, cx, cy, cz, lo, hi, planes, lane, tile):
    x_end = (lane == LANES - 1) & (tile == XT - 1)
    x_start = (lane == 0) & (tile == 0)

    def faces(first, count):
        for e in (first + r for r in range(count)):
            for z in range(planes):
                cy[e, z] = HALF * (stiff[e, z] + stiff[e + 1, z])

    def rows(first, count):
        for e in (first + r for r in range(count)):
            below = None
            following = HALF * stiff[e, 0]
            for z in range(planes):
                s = following
                face = s + jnp.where(x_end, 0.0, x_next(s, lane))
                total = face + (s + jnp.where(x_start, 0.0, x_prev(s, lane)))
                if z < NZ - 1:
                    following = HALF * stiff[e, z + 1]
                    above = s + following
                else:
                    above = s
                total = total + above + (below if z > 0 else s) + cy[e, z] + cy[e - 1, z]
                cx[e, z] = jnp.where(x_end, 0.0, face)
                cz[e, z] = above
                diag[e, z] = 2.0 - total
                below = above

    in_blocks(lo - 1, hi, 4, faces)
    in_blocks(lo, hi, 4, rows)


def leap(now, before, after, base, diag, cx, cy, cz, outer, lane, slope, inject=None):
    def cells(e, planes, slope_row):
        f = e - base
        for z in range(planes):
            u = now[f, z]
            c = cx[e, z]
            following = x_next(u, lane)
            acc = diag[e, z] * u - before[f, z]
            acc = acc + c * following + x_prev(c * u, lane)
            acc = acc + cy[e, z] * now[f + 1, z] + cy[e - 1, z] * now[f - 1, z]
            if z < NZ - 1:
                acc = acc + cz[e, z] * now[f, z + 1]
            if z > 0:
                acc = acc + cz[e, z - 1] * now[f, z - 1]
            if z == 0 and inject is not None:
                acc = acc + inject[e - OFF + EDGE]
            after[f, z] = acc
            if slope_row is not None:
                slope[slope_row, z] = following - u

    def own(i, carry):
        for r in range(4):
            cells(OFF + 4 * i + r, NZ, 4 * i + r)
        return carry

    lax.fori_loop(0, ROWS // 4, own, 0)
    for e, planes in outer:
        cells(e, planes, None)


def outer_rows(k, cone):
    whole = STEPS - k
    rows = [(OFF - whole + j, NZ) for j in range(whole)] + [(OFF + ROWS + j, NZ) for j in range(whole)]
    if cone:
        rows += [(OFF - whole - CONE + j, whole) for j in range(CONE)]
        rows += [(OFF + ROWS + whole + j, whole) for j in range(CONE)]
    return rows


def three_parts(f):
    parts = []
    for _ in range(3):
        part = f.astype(jnp.bfloat16)
        parts.append(part.astype(f32))
        f = f - parts[-1]
    return jnp.concatenate(parts, 0).astype(jnp.bfloat16)


def misfit_surfaces(waves, receivers, observed, edges, surf, lane, tile):
    column = lax.broadcasted_iota(jnp.int32, (LANES, LANES), 0)
    plan = []
    for j in range(SURF_ROWS):
        y = j - EDGE
        if y < 0:
            used, at = range(-y - 1, STEPS), edges[0][:EDGE].astype(jnp.int32)[j : j + 1]
        elif y < ROWS:
            used, at = range(STEPS), receivers[y : y + 1, :]
        else:
            used, at = range(y - ROWS, STEPS), edges[1][:EDGE].astype(jnp.int32)[y - ROWS : y - ROWS + 1]
        pick = jnp.where(column == (at & (LANES - 1)), 1.0, 0.0).astype(jnp.bfloat16)
        held = jnp.where(tile == (at >> 7), 1.0, 0.0)
        surface = jnp.concatenate([waves[k + 1][OFF + y, 0] for k in used], 0)
        lanes_of = jnp.dot(three_parts(surface), pick, preferred_element_type=f32)
        plan.append((j, used, pick, held, lanes_of))
    for j, used, pick, held, lanes_of in plan:
        y = j - EDGE
        size = len(used) * XT
        lanes_of = lanes_of[:size] + lanes_of[size : 2 * size] + lanes_of[2 * size :]
        parts = []
        for i, k in enumerate(used):
            record = jnp.sum(lanes_of[i * XT : (i + 1) * XT] * held, axis=0, keepdims=True)
            if 0 <= y < ROWS:
                trace = observed[k, y : y + 1, :]
            else:
                skip = EDGE + sum(m + 1 for m in range(k + 1, STEPS))
                r = skip + (y + k + 1 if y < 0 else y - ROWS)
                trace = edges[0 if y < 0 else 1][r : r + 1]
            parts.append(held * (record - trace))
        back = lax.dot_general(
            three_parts(jnp.concatenate(parts, 0)), pick, (((1,), (1,)), ((), ())), preferred_element_type=f32
        )
        back = back[:size] + back[size : 2 * size] + back[2 * size :]
        for i, k in enumerate(used):
            surf[k, j] = back[i * XT : (i + 1) * XT]


def forward_kernel(
    source_pos, source_wave, u0, u1, s, s_even, s_odd, s_even_other, s_odd_other, u_even, u_odd, receivers, observed,
    w1, w2, w3, w4, w5, d1, d2, d3, d4, d5, diag, cx, cy, cz, surf,
    stiff, before, edge,
):
    lane, tile = iotas()
    waves = (w1, w2, w3, w4, w5)
    slopes = (d1, d2, d3, d4)
    for ext, own in ((stiff, s), (w1, u1), (before, u0)):
        fill(ext, own, OFF)
    core = core_index()

    def stiffness_halos(low, high):
        for part, base in ((0, core * PART), (1, (1 - core) * PART)):
            for k in range(REACH):
                stiff[OFF - REACH + k, pl.ds(base, PART)] = low[part][k * PART : (k + 1) * PART]
                stiff[OFF + ROWS + k, pl.ds(base, PART)] = high[part][k * PART : (k + 1) * PART]
        fill_cone(stiff, low[0], high[0], REACH * PART, REACH)

    def wave_halos(low, high):
        fill_halo(w1, OFF, low, high, 0, REACH)
        fill_halo(before, OFF, low, high, REACH * NZ, REACH - 1)
        at = (2 * REACH - 1) * NZ
        fill_cone(w1, low, high, at, REACH)
        fill_cone(before, low, high, at + REACH * CONE, REACH - 1)
        for i, ref in enumerate((low, high)):
            edge[2 * i] = ref[TILE_U - 2]
            edge[2 * i + 1] = ref[TILE_U - 1]

    by_parity(((s_even, s_even_other), (s_odd, s_odd_other)), stiffness_halos)
    by_parity((u_even, u_odd), wave_halos)
    top, bottom = OFF - REACH, OFF + ROWS + REACH
    for lo, hi, planes in (
        (top + 1, bottom - 1, NZ),
        (top + 1 - CONE, top + 1, STEPS),
        (bottom - 1, bottom - 1 + CONE, STEPS),
    ):
        coefficients(stiff, diag, cx, cy, cz, lo, hi, planes, lane, tile)

    gy = lax.axis_index("gy")

    @pl.when(gy == 0)
    def _():
        cy[OFF - 1] = jnp.zeros((NZ, XT, LANES), f32)

    @pl.when(gy == lax.axis_size("gy") - 1)
    def _():
        cy[OFF + ROWS - 1] = jnp.zeros((NZ, XT, LANES), f32)

    z_src = source_pos[0, 0]
    e_src = source_pos[0, 1] - gy * ROWS + OFF
    x_src = source_pos[0, 2]
    spot = (tile * LANES + lane) == x_src
    for k in range(STEPS):
        older = before if k == 0 else waves[k - 1]
        after = waves[k + 1]
        leap(waves[k], older, after, 0, diag, cx, cy, cz, outer_rows(k, True), lane, slopes[k])
        reach = STEPS - k + CONE

        @pl.when((e_src >= OFF - reach) & (e_src < OFF + ROWS + reach))
        def _():
            add = jnp.where(spot, TIME_STEP_SQ * source_wave[0, k], 0.0)
            after[e_src, z_src] = after[e_src, z_src] + add

    def last_slope(i, carry):
        for y in (4 * i + r for r in range(4)):
            for z in range(NZ):
                u = w5[OFF + y, z]
                d5[y, z] = x_next(u, lane) - u
        return carry

    lax.fori_loop(0, ROWS // 4, last_slope, 0)
    edges = [jnp.concatenate([edge[2 * i], edge[2 * i + 1]], 0) for i in range(2)]
    misfit_surfaces(waves, receivers, observed, edges, surf, lane, tile)


def forward(*args):
    one = jax.ShapeDtypeStruct(FIELD, f32)
    own = jax.ShapeDtypeStruct((ROWS, NZ, XT, LANES), f32)
    surf = jax.ShapeDtypeStruct((STEPS, SURF_ROWS, XT, LANES), f32)
    outs = (one,) * (STEPS + 1) + (own,) * (STEPS + 1) + (one,) * 4 + (surf,)
    return pl.pallas_call(
        forward_kernel,
        out_shape=outs,
        in_specs=[SMEM] * 2 + [VMEM] * (len(args) - 2),
        out_specs=(VMEM,) * len(outs),
        scratch_shapes=[pltpu.VMEM(FIELD, f32)] * 2 + [pltpu.VMEM((4, XT, LANES), f32)],
        compiler_params=pltpu.CompilerParams(vmem_limit_bytes=16 << 20),
        cost_estimate=pl.CostEstimate(flops=1 << 25, bytes_accessed=1 << 24, transcendentals=0),
        name="forward",
    )(*args)


def adjoint_kernel(
    l6, l7, even, odd, w1, w2, w3, w4, w5, d1, d2, d3, d4, d5, diag, cx, cy, cz, surf,
    keep, send,
    m6, m5, m4, m3, m2, before, g6, g5, g4, g3, face_y, grad,
):
    lane, tile = iotas()
    x_end = (lane == LANES - 1) & (tile == XT - 1)
    x_side = x_end | ((lane == 0) & (tile == 0))
    lams = (m6, m5, m4, m3, m2)
    slopes = (g6, g5, g4, g3)
    fill(m6, l6, REACH)
    fill(before, l7, REACH)

    def halos(low, high):
        fill_halo(m6, REACH, low, high, 0, REACH)
        fill_halo(before, REACH, low, high, REACH * NZ, REACH - 1)

    by_parity((even, odd), halos)
    for k in range(STEPS):
        older = before if k == 0 else lams[k - 1]
        leap(
            lams[k], older, lams[k + 1], OFF - REACH, diag, cx, cy, cz, outer_rows(k, False), lane, slopes[k],
            surf.at[STEPS - 1 - k],
        )

    pairs = ((w5, m6, d5, g6), (w4, m5, d4, g5), (w3, m4, d3, g4), (w2, m3, d2, g3), (w1, m2, d1, None))
    for z in range(NZ):
        total = None
        for w, m, _, _ in pairs:
            part = (w[OFF, z] - w[OFF - 1, z]) * (m[REACH, z] - m[REACH - 1, z])
            total = part if total is None else total + part
        face_y[z] = total

    def two_rows(i, carry):
        below_y = [face_y[z] for z in range(NZ)]
        for y in (2 * i, 2 * i + 1):
            e = y + OFF
            below = None
            us = [w[e, 0] for w, _, _, _ in pairs]
            f = y + REACH
            ls = [m[f, 0] for _, m, _, _ in pairs]
            for z in range(NZ):
                fx = fy = fz = cell = None
                next_us, next_ls = [], []
                for (w, m, d, g), u, l in zip(pairs, us, ls, strict=True):
                    px = d[y, z] * (g[y, z] if g is not None else x_next(l, lane) - l)
                    py = (w[e + 1, z] - u) * (m[f + 1, z] - l)
                    both = u * l
                    if z < NZ - 1:
                        un, ln = w[e, z + 1], m[f, z + 1]
                        next_us.append(un)
                        next_ls.append(ln)
                        pz = (un - u) * (ln - l)
                    else:
                        pz = both
                    fx = px if fx is None else fx + px
                    fy = py if fy is None else fy + py
                    fz = pz if fz is None else fz + pz
                    cell = both if cell is None else cell + both
                us, ls = next_us, next_ls
                fx = jnp.where(x_end, 0.0, fx)
                total = fx + x_prev(fx, lane) + jnp.where(x_side, cell, 0.0)
                total = total + fy + below_y[z] + fz + (cell if z == 0 else below)
                below_y[z] = fy
                below = fz
                grad[z, pl.ds(y, XT, stride=ROWS), :] = -HALF * total
        for z in range(NZ):
            face_y[z] = below_y[z]
        return carry

    lax.fori_loop(0, ROWS // 2, two_rows, 0)
    core = core_index()
    for group in range(2):
        keep[group] = grad[pl.ds(8 * group + 4 * core, 4)]
        send[group] = grad[pl.ds(8 * group + 4 * (1 - core), 4)]


def adjoint(*args):
    part = jax.ShapeDtypeStruct((2, 4, XT * ROWS, LANES), f32)
    own = pltpu.VMEM((ROWS, NZ, XT, LANES), f32)
    return pl.pallas_call(
        adjoint_kernel,
        out_shape=(part, part),
        in_specs=[VMEM] * len(args),
        out_specs=(VMEM, VMEM),
        scratch_shapes=[pltpu.VMEM(SHORT, f32)] * (STEPS + 2)
        + [own] * STEPS
        + [
            pltpu.VMEM((NZ, XT, LANES), f32),
            pltpu.VMEM((NZ, XT * ROWS, LANES), f32),
        ],
        compiler_params=pltpu.CompilerParams(vmem_limit_bytes=16 << 20),
        cost_estimate=pl.CostEstimate(flops=1 << 25, bytes_accessed=1 << 24, transcendentals=0),
        name="adjoint",
    )(*args)


def finish_kernel(mine, other, out, sems):
    core = core_index()
    copies = []
    for group in range(2):
        for i, (part, base) in enumerate(((mine, core), (other, 1 - core))):
            target = out.at[pl.ds(8 * group + 4 * base, 4)]
            copies.append(pltpu.make_async_copy(part.at[group], target, sems.at[2 * group + i]))
    for copy in copies:
        copy.start()
    for copy in copies:
        copy.wait()


def finish(mine, other):
    return pl.pallas_call(
        finish_kernel,
        out_shape=jax.ShapeDtypeStruct((NZ, XT * ROWS, LANES), f32),
        in_specs=[VMEM, VMEM],
        out_specs=pl.BlockSpec(memory_space=pl.ANY),
        scratch_shapes=[pltpu.SemaphoreType.DMA((4,))],
        compiler_params=pltpu.CompilerParams(vmem_limit_bytes=2 << 20),
        name="finish",
    )(mine, other)


def swap_even(block):
    count = lax.axis_size("gy")
    pairs = [(i, i + 1) for i in range(0, count - 1, 2)]
    return lax.ppermute(block, "gy", pairs + [(j, i) for i, j in pairs])


def swap_odd(block):
    count = lax.axis_size("gy")
    pairs = [(i, i + 1) for i in range(1, count - 1, 2)]
    return lax.ppermute(block, "gy", pairs + [(j, i) for i, j in pairs])


def swap_core(block):
    return lax.ppermute(block, "shot", [(0, 1), (1, 0), (2, 3), (3, 2)])


def swap_far(block):
    return lax.ppermute(block, "shot", [(0, 2), (2, 0), (1, 3), (3, 1)])


def body(
    stiffness,
    first_moment,
    second_moment,
    wave_prev,
    wave_now,
    adjoint_next,
    adjoint_now,
    observed,
    receiver_x,
    source_pos,
    source_wave,
):
    shot = lax.axis_index("shot")
    core, far = shot % 2, shot // 2
    s = native(stiffness)
    u0, u1 = native(wave_prev[0]), native(wave_now[0])
    l6, l7 = native(adjoint_now[0]), native(adjoint_next[0])
    first, second = native(first_moment), native(second_moment)

    s_even, s_odd = pack(pack_stiffness_kernel, "pack_stiffness", TILE_S, s)
    s_even, s_odd = swap_even(s_even), swap_odd(s_odd)
    u_even, u_odd = pack(pack_waves_kernel, "pack_waves", TILE_U, u1, u0, receiver_x[0], observed[0])
    u_even, u_odd = swap_even(u_even), swap_odd(u_odd)
    s_even_other, s_odd_other = swap_core(s_even), swap_core(s_odd)
    l6_after, l7_after, s_even_other, s_odd_other = lax.optimization_barrier((l6, l7, s_even_other, s_odd_other))
    l_even, l_odd = pack(pack_adjoint_kernel, "pack_adjoint", TILE_L, l6_after, l7_after)
    l_even, l_odd = swap_even(l_even), swap_odd(l_odd)
    moments = jnp.stack([first, second])
    u_even, u_odd, moments = lax.optimization_barrier((u_even, u_odd, moments))
    moments = swap_far(moments)
    fields = forward(
        source_pos, source_wave, u0, u1, s, s_even, s_odd, s_even_other, s_odd_other, u_even, u_odd,
        receiver_x[0], observed[0],
    )
    keep, send = adjoint(l6, l7, l_even, l_odd, *fields)
    keep, send, moments = lax.optimization_barrier((keep, send, moments))
    chip_sum = keep + swap_core(send)
    share = chip_sum + swap_far(chip_sum)

    is_far = (jnp.arange(2) == far)[:, None, None, None]
    first_two = jnp.where(is_far, first[None], moments[0][None])
    second_two = jnp.where(is_far, second[None], moments[1][None])
    stiff_two = jnp.where(core == 0, s.reshape(2, 2, 4, XT * ROWS, LANES)[:, 0], s.reshape(2, 2, 4, XT * ROWS, LANES)[:, 1])
    first_new = BETA_ONE * first_two + (1.0 - BETA_ONE) * share
    second_new = BETA_TWO * second_two + (1.0 - BETA_TWO) * share * share
    updated = stiff_two - LEARN_RATE * (first_new / (1.0 - BETA_ONE**ADAM_TICKS)) / (
        jnp.sqrt(second_new / (1.0 - BETA_TWO**ADAM_TICKS)) + ADAM_EPS
    )
    other = swap_core(updated)
    stiffness_new = finish(updated, other)
    first_out = jnp.where(far == 0, first_new[0], first_new[1])
    second_out = jnp.where(far == 0, second_new[0], second_new[1])
    return (from_native(stiffness_new), from_native(first_out), from_native(second_out))


def solution(mesh):
    return jax.shard_map(
        body,
        mesh=mesh,
        in_specs=(
            P(None, "gy", None),
            P("shot", "gy", None),
            P("shot", "gy", None),
            P("shot", None, "gy", None),
            P("shot", None, "gy", None),
            P("shot", None, "gy", None),
            P("shot", None, "gy", None),
            P("shot", None, "gy", None),
            P("shot", "gy", None),
            P("shot", None),
            P("shot", None),
        ),
        out_specs=(P(None, "gy", None), P("shot", "gy", None), P("shot", "gy", None)),
        check_vma=False,
    )
```

```python
import functools

import jax
import jax.numpy as jnp
from jax import lax
from jax.experimental import pallas as pl
from jax.experimental.pallas import tpu as pltpu
from jax.sharding import PartitionSpec as P

TIME_STEP_SQ = 0.15
BETA_ONE = 0.9
BETA_TWO = 0.999
LEARN_RATE = 0.05
ADAM_EPS = 1e-08
ADAM_TICKS = 10.0

NZ = 16
ROWS = 8
XT = 8
LANES = 128
STEPS = 4
REACH = STEPS + 1
EDGE = STEPS
CONE = STEPS - 1
OFF = ROWS
EXT = ROWS + 2 * OFF
FIELD = (EXT, NZ, XT, LANES)
SHORT = (ROWS + 2 * REACH, NZ, XT, LANES)
SURF_ROWS = ROWS + 2 * EDGE
PART = NZ // 2
TIP = CONE * (CONE + 1) // 2
TILE_S = REACH * PART + TIP
TILE_U = (2 * REACH - 1) * NZ + 2 * TIP + 2
TILE_A = TILE_S + TILE_U
TILE_L = (2 * REACH - 1) * NZ
HALF = 0.5 * TIME_STEP_SQ
PACK_VMEM = 56 << 20

f32 = jnp.float32
VMEM = pl.BlockSpec(memory_space=pltpu.VMEM)
SMEM = pl.BlockSpec(memory_space=pltpu.SMEM)


def native(block):
    planes = block.shape[0]
    return block.reshape(planes, ROWS, XT, LANES).transpose(0, 2, 1, 3).reshape(planes, XT * ROWS, LANES)


def from_native(block):
    planes = block.shape[0]
    return block.reshape(planes, XT, ROWS, LANES).transpose(0, 2, 1, 3).reshape(planes, ROWS, XT * LANES)


def row_of(ref, z, y):
    return ref[z, pl.ds(y, XT, stride=ROWS), :]


def x_next(f, lane):
    r = pltpu.roll(f, LANES - 1, 1)
    return jnp.where(lane == LANES - 1, pltpu.roll(r, XT - 1, 0), r)


def x_prev(f, lane):
    r = pltpu.roll(f, 1, 1)
    return jnp.where(lane == 0, pltpu.roll(r, 1, 0), r)


def iotas():
    lane = lax.broadcasted_iota(jnp.int32, (XT, LANES), 1)
    tile = lax.broadcasted_iota(jnp.int32, (XT, LANES), 0)
    return lane, tile


def in_blocks(lo, hi, size, rows):
    whole = (hi - lo) // size
    if whole:
        lax.fori_loop(0, whole, lambda i, c: (rows(lo + i * size, size), c)[1], 0)
    if (hi - lo) % size:
        rows(lo + whole * size, (hi - lo) % size)


def pack_fields(fields, widths, low, high, at):
    def plane(z, carry):
        first = at
        for ref, width in zip(fields, widths, strict=True):
            for k in range(width):
                low[first + k * NZ + z] = row_of(ref, z, k)
                high[first + k * NZ + z] = row_of(ref, z, ROWS - width + k)
            first += width * NZ
        return carry

    lax.fori_loop(0, NZ, plane, 0)
    return at + sum(widths) * NZ


def core_index():
    return lax.rem(lax.axis_index("shot"), 2)


def by_parity(pair, work):
    parity = lax.rem(lax.axis_index("gy"), 2)

    @pl.when(parity == 0)
    def _():
        work(pair[1], pair[0])

    @pl.when(parity == 1)
    def _():
        work(pair[0], pair[1])


def pack_cone(ref, width, low, high, at):
    for k in range(CONE):
        for z in range(CONE - k):
            low[at] = row_of(ref, z, width + k)
            high[at] = row_of(ref, z, ROWS - 1 - width - k)
            at += 1
    return at


def fetch(sources, places, sems):
    copies = [pltpu.make_async_copy(a, b, sems.at[i]) for i, (a, b) in enumerate(zip(sources, places, strict=True))]
    for copy in copies:
        copy.start()
    for copy in copies:
        copy.wait()


def pack_first_kernel(
    s_far, u1_far, u0_far, receivers_far, observed_far, even, odd, s, u1, u0, receivers, observed, sems
):
    fetch((s_far, u1_far, u0_far, receivers_far, observed_far), (s, u1, u0, receivers, observed), sems)
    base = core_index() * PART

    def work(low, high):
        def plane(z, carry):
            for k in range(REACH):
                low[k * PART + z] = row_of(s, base + z, k)
                high[k * PART + z] = row_of(s, base + z, ROWS - REACH + k)
            return carry

        lax.fori_loop(0, PART, plane, 0)
        at = pack_cone(s, REACH, low, high, REACH * PART)
        at = pack_fields((u1, u0), (REACH, REACH - 1), low, high, at)
        at = pack_cone(u1, REACH, low, high, at)
        at = pack_cone(u0, REACH - 1, low, high, at)
        where = receivers[...].astype(f32)
        empty = jnp.zeros((2, LANES), f32)
        for side, rows in ((low, lambda n: slice(0, n)), (high, lambda n: slice(ROWS - n, ROWS))):
            parts = [where[rows(EDGE)]]
            for k in range(STEPS - 1, -1, -1):
                parts.append(observed[k][rows(k + 1)])
            parts.append(empty)
            both = jnp.concatenate(parts, 0)
            side[at] = both[:XT]
            side[at + 1] = both[XT:]

    by_parity((even, odd), work)


def pack_adjoint_kernel(l6_far, l7_far, even, odd, l6, l7, sems):
    fetch((l6_far, l7_far), (l6, l7), sems)
    by_parity((even, odd), lambda low, high: pack_fields((l6, l7), (REACH, REACH - 1), low, high, 0))


def pack(kernel, name, tiles, *arrays):
    shape = pltpu.VMEM((tiles, XT, LANES), f32)
    return pl.pallas_call(
        kernel,
        out_shape=(shape, shape),
        in_specs=[pl.BlockSpec(memory_space=pl.ANY)] * len(arrays),
        out_specs=(VMEM, VMEM),
        scratch_shapes=[pltpu.VMEM(a.shape, a.dtype) for a in arrays] + [pltpu.SemaphoreType.DMA((len(arrays),))],
        compiler_params=pltpu.CompilerParams(vmem_limit_bytes=PACK_VMEM),
        cost_estimate=pl.CostEstimate(flops=0, bytes_accessed=1 << 16, transcendentals=0),
        name=name,
    )(*arrays)


def fill(ext, own, off):
    def plane(z, carry):
        for k in range(ROWS):
            ext[off + k, z] = row_of(own, z, k)
        return carry

    lax.fori_loop(0, NZ, plane, 0)


def fill_halo(ext, off, low, high, at, width):
    for k in range(width):
        ext[off - width + k] = low[at + k * NZ : at + (k + 1) * NZ]
        ext[off + ROWS + k] = high[at + k * NZ : at + (k + 1) * NZ]


def fill_cone(ext, low, high, at, width):
    for k in range(CONE):
        planes = CONE - k
        ext[OFF - 1 - width - k, :planes] = low[at : at + planes]
        ext[OFF + ROWS + width + k, :planes] = high[at : at + planes]
        at += planes


def coefficients(stiff, diag, cx, cy, cz, lane, tile):
    x_end = (lane == LANES - 1) & (tile == XT - 1)
    x_start = (lane == 0) & (tile == 0)
    top, bottom = OFF - REACH, OFF + ROWS + REACH

    def face_y(e, planes):
        for z in range(planes):
            cy[e, z] = HALF * (stiff[e, z] + stiff[e + 1, z])

    def cells(e, planes):
        below = None
        following = HALF * stiff[e, 0]
        for z in range(planes):
            s = following
            face = s + jnp.where(x_end, 0.0, x_next(s, lane))
            total = face + (s + jnp.where(x_start, 0.0, x_prev(s, lane)))
            if z < NZ - 1:
                following = HALF * stiff[e, z + 1]
                above = s + following
            else:
                above = s
            total = total + above + (below if z > 0 else s) + cy[e, z] + cy[e - 1, z]
            cx[e, z] = jnp.where(x_end, 0.0, face)
            cz[e, z] = above
            diag[e, z] = 2.0 - total
            below = above

    def faces(first, count):
        for r in range(count):
            face_y(first + r, NZ)

    def rows(first, count):
        for r in range(count):
            cells(first + r, NZ)

    in_blocks(top, bottom - 1, 4, faces)
    for k in range(CONE):
        face_y(top - 1 - k, CONE - k)
        face_y(bottom - 1 + k, CONE - k)
    in_blocks(top + 1, bottom - 1, 4, rows)
    for k in range(CONE):
        cells(top - k, CONE - k)
        cells(bottom - 1 + k, CONE - k)


def leap(now, before, after, base, diag, cx, cy, cz, outer, lane, slope, inject=None):
    def cells(e, planes, slope_row):
        f = e - base
        for z in range(planes):
            u = now[f, z]
            c = cx[e, z]
            following = x_next(u, lane)
            acc = diag[e, z] * u - before[f, z]
            acc = acc + c * following + x_prev(c * u, lane)
            acc = acc + cy[e, z] * now[f + 1, z] + cy[e - 1, z] * now[f - 1, z]
            if z < NZ - 1:
                acc = acc + cz[e, z] * now[f, z + 1]
            if z > 0:
                acc = acc + cz[e, z - 1] * now[f, z - 1]
            if z == 0 and inject is not None:
                acc = acc + inject[e - OFF + EDGE]
            after[f, z] = acc
            if slope_row is not None:
                slope[slope_row, z] = following - u

    for r in range(ROWS):
        cells(OFF + r, NZ, r)
    for e, planes in outer:
        cells(e, planes, None)


def outer_rows(k, cone):
    whole = STEPS - k
    rows = [(OFF - whole + j, NZ) for j in range(whole)] + [(OFF + ROWS + j, NZ) for j in range(whole)]
    if cone:
        for j in range(CONE):
            planes = min(CONE - j, whole)
            rows += [(OFF - 1 - whole - j, planes), (OFF + ROWS + whole + j, planes)]
    return rows


def three_parts(f):
    parts = []
    for _ in range(3):
        part = f.astype(jnp.bfloat16)
        parts.append(part.astype(f32))
        f = f - parts[-1]
    return jnp.concatenate(parts, 0).astype(jnp.bfloat16)


def misfit_surfaces(waves, receivers, observed, edges, surf, lane, tile):
    column = lax.broadcasted_iota(jnp.int32, (LANES, LANES), 0)
    plan = []
    for j in range(SURF_ROWS):
        y = j - EDGE
        if y < 0:
            used, at = range(-y - 1, STEPS), edges[0][:EDGE].astype(jnp.int32)[j : j + 1]
        elif y < ROWS:
            used, at = range(STEPS), receivers[y : y + 1, :]
        else:
            used, at = range(y - ROWS, STEPS), edges[1][:EDGE].astype(jnp.int32)[y - ROWS : y - ROWS + 1]
        pick = jnp.where(column == (at & (LANES - 1)), 1.0, 0.0).astype(jnp.bfloat16)
        held = jnp.where(tile == (at >> 7), 1.0, 0.0)
        surface = jnp.concatenate([waves[k + 1][OFF + y, 0] for k in used], 0)
        lanes_of = jnp.dot(three_parts(surface), pick, preferred_element_type=f32)
        plan.append((j, used, pick, held, lanes_of))
    for j, used, pick, held, lanes_of in plan:
        y = j - EDGE
        size = len(used) * XT
        lanes_of = lanes_of[:size] + lanes_of[size : 2 * size] + lanes_of[2 * size :]
        parts = []
        for i, k in enumerate(used):
            record = jnp.sum(lanes_of[i * XT : (i + 1) * XT] * held, axis=0, keepdims=True)
            if 0 <= y < ROWS:
                trace = observed[k, y : y + 1, :]
            else:
                skip = EDGE + sum(m + 1 for m in range(k + 1, STEPS))
                r = skip + (y + k + 1 if y < 0 else y - ROWS)
                trace = edges[0 if y < 0 else 1][r : r + 1]
            parts.append(held * (record - trace))
        back = lax.dot_general(
            three_parts(jnp.concatenate(parts, 0)), pick, (((1,), (1,)), ((), ())), preferred_element_type=f32
        )
        back = back[:size] + back[size : 2 * size] + back[2 * size :]
        for i, k in enumerate(used):
            surf[k, j] = back[i * XT : (i + 1) * XT]


def forward_kernel(
    source_pos, source_wave, u0, u1, s, even, odd, even_other, odd_other, receivers, observed,
    w1, w2, w3, w4, w5, d1, d2, d3, d4, d5, diag, cx, cy, cz, surf,
    stiff, before, edge,
):
    lane, tile = iotas()
    waves = (w1, w2, w3, w4, w5)
    slopes = (d1, d2, d3, d4)
    for ext, own in ((stiff, s), (w1, u1), (before, u0)):
        fill(ext, own, OFF)
    core = core_index()

    def halos(low, high):
        for part, base in ((0, core * PART), (1, (1 - core) * PART)):
            for k in range(REACH):
                stiff[OFF - REACH + k, pl.ds(base, PART)] = low[part][k * PART : (k + 1) * PART]
                stiff[OFF + ROWS + k, pl.ds(base, PART)] = high[part][k * PART : (k + 1) * PART]
        low, high = low[0], high[0]
        fill_cone(stiff, low, high, REACH * PART, REACH)
        at = TILE_S
        fill_halo(w1, OFF, low, high, at, REACH)
        at += REACH * NZ
        fill_halo(before, OFF, low, high, at, REACH - 1)
        at += (REACH - 1) * NZ
        fill_cone(w1, low, high, at, REACH)
        fill_cone(before, low, high, at + TIP, REACH - 1)
        for i, ref in enumerate((low, high)):
            edge[2 * i] = ref[TILE_A - 2]
            edge[2 * i + 1] = ref[TILE_A - 1]

    by_parity(((even, even_other), (odd, odd_other)), halos)
    coefficients(stiff, diag, cx, cy, cz, lane, tile)
    gy = lax.axis_index("gy")

    @pl.when(gy == 0)
    def _():
        cy[OFF - 1] = jnp.zeros((NZ, XT, LANES), f32)

    @pl.when(gy == lax.axis_size("gy") - 1)
    def _():
        cy[OFF + ROWS - 1] = jnp.zeros((NZ, XT, LANES), f32)

    z_src = source_pos[0, 0]
    e_src = source_pos[0, 1] - gy * ROWS + OFF
    x_src = source_pos[0, 2]
    spot = (tile * LANES + lane) == x_src
    for k in range(STEPS):
        older = before if k == 0 else waves[k - 1]
        after = waves[k + 1]
        leap(waves[k], older, after, 0, diag, cx, cy, cz, outer_rows(k, True), lane, slopes[k])
        reach = STEPS - k + CONE

        @pl.when((e_src >= OFF - reach) & (e_src < OFF + ROWS + reach))
        def _():
            add = jnp.where(spot, TIME_STEP_SQ * source_wave[0, k], 0.0)
            after[e_src, z_src] = after[e_src, z_src] + add

    def last_slope(i, carry):
        for y in (4 * i + r for r in range(4)):
            for z in range(NZ):
                u = w5[OFF + y, z]
                d5[y, z] = x_next(u, lane) - u
        return carry

    lax.fori_loop(0, ROWS // 4, last_slope, 0)
    edges = [jnp.concatenate([edge[2 * i], edge[2 * i + 1]], 0) for i in range(2)]
    misfit_surfaces(waves, receivers, observed, edges, surf, lane, tile)


def forward(*args):
    one = jax.ShapeDtypeStruct(FIELD, f32)
    own = jax.ShapeDtypeStruct((ROWS, NZ, XT, LANES), f32)
    surf = jax.ShapeDtypeStruct((STEPS, SURF_ROWS, XT, LANES), f32)
    outs = (one,) * (STEPS + 1) + (own,) * (STEPS + 1) + (one,) * 4 + (surf,)
    return pl.pallas_call(
        forward_kernel,
        out_shape=outs,
        in_specs=[SMEM] * 2 + [VMEM] * (len(args) - 2),
        out_specs=(VMEM,) * len(outs),
        scratch_shapes=[pltpu.VMEM(FIELD, f32)] * 2 + [pltpu.VMEM((4, XT, LANES), f32)],
        compiler_params=pltpu.CompilerParams(vmem_limit_bytes=16 << 20),
        cost_estimate=pl.CostEstimate(flops=1 << 25, bytes_accessed=1 << 24, transcendentals=0),
        name="forward",
    )(*args)


def adjoint_kernel(
    l6, l7, even, odd, w1, w2, w3, w4, w5, d1, d2, d3, d4, d5, diag, cx, cy, cz, surf,
    keep, send,
    m6, m5, m4, m3, m2, before, g6, g5, g4, g3, face_y, grad,
):
    lane, tile = iotas()
    x_end = (lane == LANES - 1) & (tile == XT - 1)
    x_side = x_end | ((lane == 0) & (tile == 0))
    lams = (m6, m5, m4, m3, m2)
    slopes = (g6, g5, g4, g3)
    fill(m6, l6, REACH)
    fill(before, l7, REACH)

    def halos(low, high):
        fill_halo(m6, REACH, low, high, 0, REACH)
        fill_halo(before, REACH, low, high, REACH * NZ, REACH - 1)

    by_parity((even, odd), halos)
    for k in range(STEPS):
        older = before if k == 0 else lams[k - 1]
        leap(
            lams[k], older, lams[k + 1], OFF - REACH, diag, cx, cy, cz, outer_rows(k, False), lane, slopes[k],
            surf.at[STEPS - 1 - k],
        )

    pairs = ((w5, m6, d5, g6), (w4, m5, d4, g5), (w3, m4, d3, g4), (w2, m3, d2, g3), (w1, m2, d1, None))
    for z in range(NZ):
        total = None
        for w, m, _, _ in pairs:
            part = (w[OFF, z] - w[OFF - 1, z]) * (m[REACH, z] - m[REACH - 1, z])
            total = part if total is None else total + part
        face_y[z] = total

    def two_rows(i, carry):
        below_y = [face_y[z] for z in range(NZ)]
        for y in (2 * i, 2 * i + 1):
            e = y + OFF
            below = None
            us = [w[e, 0] for w, _, _, _ in pairs]
            f = y + REACH
            ls = [m[f, 0] for _, m, _, _ in pairs]
            for z in range(NZ):
                fx = fy = fz = cell = None
                next_us, next_ls = [], []
                for (w, m, d, g), u, l in zip(pairs, us, ls, strict=True):
                    px = d[y, z] * (g[y, z] if g is not None else x_next(l, lane) - l)
                    py = (w[e + 1, z] - u) * (m[f + 1, z] - l)
                    both = u * l
                    if z < NZ - 1:
                        un, ln = w[e, z + 1], m[f, z + 1]
                        next_us.append(un)
                        next_ls.append(ln)
                        pz = (un - u) * (ln - l)
                    else:
                        pz = both
                    fx = px if fx is None else fx + px
                    fy = py if fy is None else fy + py
                    fz = pz if fz is None else fz + pz
                    cell = both if cell is None else cell + both
                us, ls = next_us, next_ls
                fx = jnp.where(x_end, 0.0, fx)
                total = fx + x_prev(fx, lane) + jnp.where(x_side, cell, 0.0)
                total = total + fy + below_y[z] + fz + (cell if z == 0 else below)
                below_y[z] = fy
                below = fz
                grad[z, pl.ds(y, XT, stride=ROWS), :] = -HALF * total
        for z in range(NZ):
            face_y[z] = below_y[z]
        return carry

    lax.fori_loop(0, ROWS // 2, two_rows, 0)
    core = core_index()
    for group in range(2):
        keep[group] = grad[pl.ds(8 * group + 4 * core, 4)]
        send[group] = grad[pl.ds(8 * group + 4 * (1 - core), 4)]


def adjoint(*args):
    part = jax.ShapeDtypeStruct((2, 4, XT * ROWS, LANES), f32)
    own = pltpu.VMEM((ROWS, NZ, XT, LANES), f32)
    return pl.pallas_call(
        adjoint_kernel,
        out_shape=(part, part),
        in_specs=[VMEM] * len(args),
        out_specs=(VMEM, VMEM),
        scratch_shapes=[pltpu.VMEM(SHORT, f32)] * (STEPS + 2)
        + [own] * STEPS
        + [
            pltpu.VMEM((NZ, XT, LANES), f32),
            pltpu.VMEM((NZ, XT * ROWS, LANES), f32),
        ],
        compiler_params=pltpu.CompilerParams(vmem_limit_bytes=16 << 20),
        cost_estimate=pl.CostEstimate(flops=1 << 25, bytes_accessed=1 << 24, transcendentals=0),
        name="adjoint",
    )(*args)


def finish_kernel(mine, other, out, sems):
    core = core_index()
    copies = []
    for group in range(2):
        for i, (part, base) in enumerate(((mine, core), (other, 1 - core))):
            target = out.at[pl.ds(8 * group + 4 * base, 4)]
            copies.append(pltpu.make_async_copy(part.at[group], target, sems.at[2 * group + i]))
    for copy in copies:
        copy.start()
    for copy in copies:
        copy.wait()


def finish(mine, other):
    return pl.pallas_call(
        finish_kernel,
        out_shape=jax.ShapeDtypeStruct((NZ, XT * ROWS, LANES), f32),
        in_specs=[VMEM, VMEM],
        out_specs=pl.BlockSpec(memory_space=pl.ANY),
        scratch_shapes=[pltpu.SemaphoreType.DMA((4,))],
        compiler_params=pltpu.CompilerParams(vmem_limit_bytes=2 << 20),
        name="finish",
    )(mine, other)


def swap_even(block):
    count = lax.axis_size("gy")
    pairs = [(i, i + 1) for i in range(0, count - 1, 2)]
    return lax.ppermute(block, "gy", pairs + [(j, i) for i, j in pairs])


def swap_odd(block):
    count = lax.axis_size("gy")
    pairs = [(i, i + 1) for i in range(1, count - 1, 2)]
    return lax.ppermute(block, "gy", pairs + [(j, i) for i, j in pairs])


def swap_core(block):
    return lax.ppermute(block, "shot", [(0, 1), (1, 0), (2, 3), (3, 2)])


def swap_far(block):
    return lax.ppermute(block, "shot", [(0, 2), (2, 0), (1, 3), (3, 1)])


def body(
    stiffness,
    first_moment,
    second_moment,
    wave_prev,
    wave_now,
    adjoint_next,
    adjoint_now,
    observed,
    receiver_x,
    source_pos,
    source_wave,
):
    shot = lax.axis_index("shot")
    core, far = shot % 2, shot // 2
    s = native(stiffness)
    u0, u1 = native(wave_prev[0]), native(wave_now[0])
    l6, l7 = native(adjoint_now[0]), native(adjoint_next[0])
    first, second = native(first_moment), native(second_moment)

    a_even, a_odd = pack(pack_first_kernel, "pack_first", TILE_A, s, u1, u0, receiver_x[0], observed[0])
    l_even, l_odd = pack(pack_adjoint_kernel, "pack_adjoint", TILE_L, l6, l7)
    a_even, a_odd = swap_even(a_even), swap_odd(a_odd)
    l_even, l_odd, a_even = lax.optimization_barrier((l_even, l_odd, a_even))
    l_even, l_odd = swap_even(l_even), swap_odd(l_odd)
    even_other, odd_other = swap_core(a_even[:TILE_S]), swap_core(a_odd[:TILE_S])
    *fields, surf = forward(
        source_pos, source_wave, u0, u1, s, a_even, a_odd, even_other, odd_other, receiver_x[0], observed[0]
    )
    moments = jnp.stack([first, second])
    l_even, moments, surf = lax.optimization_barrier((l_even, moments, surf))
    moments = swap_far(moments)
    keep, send = adjoint(l6, l7, l_even, l_odd, *fields, surf)
    keep, send, moments = lax.optimization_barrier((keep, send, moments))
    chip_sum = keep + swap_core(send)
    share = chip_sum + swap_far(chip_sum)
    first_two = jnp.where(far == 0, jnp.stack([first, moments[0]]), jnp.stack([moments[0], first]))
    second_two = jnp.where(far == 0, jnp.stack([second, moments[1]]), jnp.stack([moments[1], second]))
    halves = s.reshape(2, 2, 4, XT * ROWS, LANES)
    stiff_two = jnp.where(core == 0, halves[:, 0], halves[:, 1])
    first_new = BETA_ONE * first_two + (1.0 - BETA_ONE) * share
    second_new = BETA_TWO * second_two + (1.0 - BETA_TWO) * share * share
    updated = stiff_two - LEARN_RATE * (first_new / (1.0 - BETA_ONE**ADAM_TICKS)) / (
        jnp.sqrt(second_new / (1.0 - BETA_TWO**ADAM_TICKS)) + ADAM_EPS
    )
    stiffness_new = finish(updated, swap_core(updated))
    first_new = jnp.where(far == 0, first_new[0], first_new[1])
    second_new = jnp.where(far == 0, second_new[0], second_new[1])
    return (from_native(stiffness_new), from_native(first_new), from_native(second_new))


def solution(mesh):
    return jax.shard_map(
        body,
        mesh=mesh,
        in_specs=(
            P(None, "gy", None),
            P("shot", "gy", None),
            P("shot", "gy", None),
            P("shot", None, "gy", None),
            P("shot", None, "gy", None),
            P("shot", None, "gy", None),
            P("shot", None, "gy", None),
            P("shot", None, "gy", None),
            P("shot", "gy", None),
            P("shot", None),
            P("shot", None),
        ),
        out_specs=(P(None, "gy", None), P("shot", "gy", None), P("shot", "gy", None)),
        check_vma=False,
    )
```

```python
import functools

import jax
import jax.numpy as jnp
from jax import lax
from jax.experimental import pallas as pl
from jax.experimental.pallas import tpu as pltpu
from jax.sharding import PartitionSpec as P

TIME_STEP_SQ = 0.15
BETA_ONE = 0.9
BETA_TWO = 0.999
LEARN_RATE = 0.05
ADAM_EPS = 1e-08
ADAM_TICKS = 10.0

NZ = 16
ROWS = 8
XT = 8
LANES = 128
STEPS = 4
REACH = STEPS + 1
EDGE = STEPS
CONE = STEPS - 1
OFF = ROWS
EXT = ROWS + 2 * OFF
FIELD = (EXT, NZ, XT, LANES)
SHORT = (ROWS + 2 * REACH, NZ, XT, LANES)
SURF_ROWS = ROWS + 2 * EDGE
PART = NZ // 2
TIP = CONE * (CONE + 1) // 2
TILE_S = REACH * PART + TIP
TILE_U = (2 * REACH - 1) * NZ + 2 * TIP + 2
TILE_A = TILE_S + TILE_U
TILE_L = (2 * REACH - 1) * NZ
HALF = 0.5 * TIME_STEP_SQ
PACK_VMEM = 56 << 20

f32 = jnp.float32
VMEM = pl.BlockSpec(memory_space=pltpu.VMEM)
SMEM = pl.BlockSpec(memory_space=pltpu.SMEM)


def native(block):
    planes = block.shape[0]
    return block.reshape(planes, ROWS, XT, LANES).transpose(0, 2, 1, 3).reshape(planes, XT * ROWS, LANES)


def from_native(block):
    planes = block.shape[0]
    return block.reshape(planes, XT, ROWS, LANES).transpose(0, 2, 1, 3).reshape(planes, ROWS, XT * LANES)


def row_of(ref, z, y):
    return ref[z, pl.ds(y, XT, stride=ROWS), :]


def x_next(f, lane):
    r = pltpu.roll(f, LANES - 1, 1)
    return jnp.where(lane == LANES - 1, pltpu.roll(r, XT - 1, 0), r)


def x_prev(f, lane):
    r = pltpu.roll(f, 1, 1)
    return jnp.where(lane == 0, pltpu.roll(r, 1, 0), r)


def iotas():
    lane = lax.broadcasted_iota(jnp.int32, (XT, LANES), 1)
    tile = lax.broadcasted_iota(jnp.int32, (XT, LANES), 0)
    return lane, tile


def in_blocks(lo, hi, size, rows):
    whole = (hi - lo) // size
    if whole:
        lax.fori_loop(0, whole, lambda i, c: (rows(lo + i * size, size), c)[1], 0)
    if (hi - lo) % size:
        rows(lo + whole * size, (hi - lo) % size)


def pack_fields(fields, widths, low, high, at):
    def plane(z, carry):
        first = at
        for ref, width in zip(fields, widths, strict=True):
            for k in range(width):
                low[first + k * NZ + z] = row_of(ref, z, k)
                high[first + k * NZ + z] = row_of(ref, z, ROWS - width + k)
            first += width * NZ
        return carry

    lax.fori_loop(0, NZ, plane, 0)
    return at + sum(widths) * NZ


def core_index():
    return lax.rem(lax.axis_index("shot"), 2)


def by_parity(pair, work):
    parity = lax.rem(lax.axis_index("gy"), 2)

    @pl.when(parity == 0)
    def _():
        work(pair[1], pair[0])

    @pl.when(parity == 1)
    def _():
        work(pair[0], pair[1])


def pack_cone(ref, width, low, high, at):
    for k in range(CONE):
        for z in range(CONE - k):
            low[at] = row_of(ref, z, width + k)
            high[at] = row_of(ref, z, ROWS - 1 - width - k)
            at += 1
    return at


def fetch(sources, places, sems):
    copies = [pltpu.make_async_copy(a, b, sems.at[i]) for i, (a, b) in enumerate(zip(sources, places, strict=True))]
    for copy in copies:
        copy.start()
    for copy in copies:
        copy.wait()


def pack_first_kernel(
    s_far, u1_far, u0_far, receivers_far, observed_far, even, odd, s, u1, u0, receivers, observed, sems
):
    fetch((s_far, u1_far, u0_far, receivers_far, observed_far), (s, u1, u0, receivers, observed), sems)
    base = core_index() * PART

    def work(low, high):
        def plane(z, carry):
            for k in range(REACH):
                low[k * PART + z] = row_of(s, base + z, k)
                high[k * PART + z] = row_of(s, base + z, ROWS - REACH + k)
            return carry

        lax.fori_loop(0, PART, plane, 0)
        at = pack_cone(s, REACH, low, high, REACH * PART)
        at = pack_fields((u1, u0), (REACH, REACH - 1), low, high, at)
        at = pack_cone(u1, REACH, low, high, at)
        at = pack_cone(u0, REACH - 1, low, high, at)
        where = receivers[...].astype(f32)
        empty = jnp.zeros((2, LANES), f32)
        for side, rows in ((low, lambda n: slice(0, n)), (high, lambda n: slice(ROWS - n, ROWS))):
            parts = [where[rows(EDGE)]]
            for k in range(STEPS - 1, -1, -1):
                parts.append(observed[k][rows(k + 1)])
            parts.append(empty)
            both = jnp.concatenate(parts, 0)
            side[at] = both[:XT]
            side[at + 1] = both[XT:]

    by_parity((even, odd), work)


def pack_adjoint_kernel(l6_far, l7_far, even, odd, l6, l7, sems):
    fetch((l6_far, l7_far), (l6, l7), sems)
    by_parity((even, odd), lambda low, high: pack_fields((l6, l7), (REACH, REACH - 1), low, high, 0))


def pack(kernel, name, tiles, *arrays):
    shape = pltpu.VMEM((tiles, XT, LANES), f32)
    return pl.pallas_call(
        kernel,
        out_shape=(shape, shape),
        in_specs=[pl.BlockSpec(memory_space=pl.ANY)] * len(arrays),
        out_specs=(VMEM, VMEM),
        scratch_shapes=[pltpu.VMEM(a.shape, a.dtype) for a in arrays] + [pltpu.SemaphoreType.DMA((len(arrays),))],
        compiler_params=pltpu.CompilerParams(vmem_limit_bytes=PACK_VMEM),
        cost_estimate=pl.CostEstimate(flops=0, bytes_accessed=1 << 16, transcendentals=0),
        name=name,
    )(*arrays)


def fill(ext, own, off):
    def plane(z, carry):
        for k in range(ROWS):
            ext[off + k, z] = row_of(own, z, k)
        return carry

    lax.fori_loop(0, NZ, plane, 0)


def fill_halo(ext, off, low, high, at, width):
    for k in range(width):
        ext[off - width + k] = low[at + k * NZ : at + (k + 1) * NZ]
        ext[off + ROWS + k] = high[at + k * NZ : at + (k + 1) * NZ]


def fill_cone(ext, low, high, at, width):
    for k in range(CONE):
        planes = CONE - k
        ext[OFF - 1 - width - k, :planes] = low[at : at + planes]
        ext[OFF + ROWS + width + k, :planes] = high[at : at + planes]
        at += planes


def coefficients(stiff, diag, cx, cy, cz, lane, tile):
    x_end = (lane == LANES - 1) & (tile == XT - 1)
    x_start = (lane == 0) & (tile == 0)
    top, bottom = OFF - REACH, OFF + ROWS + REACH

    def face_y(e, planes):
        for z in range(planes):
            cy[e, z] = HALF * (stiff[e, z] + stiff[e + 1, z])

    def cells(e, planes):
        below = None
        following = HALF * stiff[e, 0]
        for z in range(planes):
            s = following
            face = s + jnp.where(x_end, 0.0, x_next(s, lane))
            total = face + (s + jnp.where(x_start, 0.0, x_prev(s, lane)))
            if z < NZ - 1:
                following = HALF * stiff[e, z + 1]
                above = s + following
            else:
                above = s
            total = total + above + (below if z > 0 else s) + cy[e, z] + cy[e - 1, z]
            cx[e, z] = jnp.where(x_end, 0.0, face)
            cz[e, z] = above
            diag[e, z] = 2.0 - total
            below = above

    def faces(first, count):
        for r in range(count):
            face_y(first + r, NZ)

    def rows(first, count):
        for r in range(count):
            cells(first + r, NZ)

    in_blocks(top, bottom - 1, 4, faces)
    for k in range(CONE):
        face_y(top - 1 - k, CONE - k)
        face_y(bottom - 1 + k, CONE - k)
    in_blocks(top + 1, bottom - 1, 4, rows)
    for k in range(CONE):
        cells(top - k, CONE - k)
        cells(bottom - 1 + k, CONE - k)


def leap(now, before, after, base, diag, cx, cy, cz, rows, lane, slope, inject=None):
    for e, planes in rows:
        f = e - base
        for z in range(planes):
            u = now[f, z]
            c = cx[e, z]
            following = x_next(u, lane)
            acc = diag[e, z] * u - before[f, z]
            acc = acc + c * following + x_prev(c * u, lane)
            acc = acc + cy[e, z] * now[f + 1, z] + cy[e - 1, z] * now[f - 1, z]
            if z < NZ - 1:
                acc = acc + cz[e, z] * now[f, z + 1]
            if z > 0:
                acc = acc + cz[e, z - 1] * now[f, z - 1]
            if z == 0 and inject is not None:
                acc = acc + inject[e - OFF + EDGE]
            after[f, z] = acc
            if OFF <= e < OFF + ROWS:
                slope[e - OFF, z] = following - u


def inner_rows(k):
    return [(OFF + y, NZ) for y in range(k + 1, ROWS - 1 - k)]


def step_rows(k, cone, skip=()):
    whole = STEPS - k
    rows = [(OFF + y, NZ) for y in range(ROWS)]
    rows += [(OFF - whole + j, NZ) for j in range(whole)] + [(OFF + ROWS + j, NZ) for j in range(whole)]
    if cone:
        for j in range(CONE):
            planes = min(CONE - j, whole)
            rows += [(OFF - 1 - whole - j, planes), (OFF + ROWS + whole + j, planes)]
    return [row for row in rows if row not in skip]


def three_parts(f):
    parts = []
    for _ in range(3):
        part = f.astype(jnp.bfloat16)
        parts.append(part.astype(f32))
        f = f - parts[-1]
    return jnp.concatenate(parts, 0).astype(jnp.bfloat16)


def misfit_surfaces(waves, receivers, observed, edges, surf, lane, tile):
    column = lax.broadcasted_iota(jnp.int32, (LANES, LANES), 0)
    plan = []
    for j in range(SURF_ROWS):
        y = j - EDGE
        if y < 0:
            used, at = range(-y - 1, STEPS), edges[0][:EDGE].astype(jnp.int32)[j : j + 1]
        elif y < ROWS:
            used, at = range(STEPS), receivers[y : y + 1, :]
        else:
            used, at = range(y - ROWS, STEPS), edges[1][:EDGE].astype(jnp.int32)[y - ROWS : y - ROWS + 1]
        pick = jnp.where(column == (at & (LANES - 1)), 1.0, 0.0).astype(jnp.bfloat16)
        held = jnp.where(tile == (at >> 7), 1.0, 0.0)
        surface = jnp.concatenate([waves[k + 1][OFF + y, 0] for k in used], 0)
        lanes_of = jnp.dot(three_parts(surface), pick, preferred_element_type=f32)
        plan.append((j, used, pick, held, lanes_of))
    for j, used, pick, held, lanes_of in plan:
        y = j - EDGE
        size = len(used) * XT
        lanes_of = lanes_of[:size] + lanes_of[size : 2 * size] + lanes_of[2 * size :]
        parts = []
        for i, k in enumerate(used):
            record = jnp.sum(lanes_of[i * XT : (i + 1) * XT] * held, axis=0, keepdims=True)
            if 0 <= y < ROWS:
                trace = observed[k, y : y + 1, :]
            else:
                skip = EDGE + sum(m + 1 for m in range(k + 1, STEPS))
                r = skip + (y + k + 1 if y < 0 else y - ROWS)
                trace = edges[0 if y < 0 else 1][r : r + 1]
            parts.append(held * (record - trace))
        back = lax.dot_general(
            three_parts(jnp.concatenate(parts, 0)), pick, (((1,), (1,)), ((), ())), preferred_element_type=f32
        )
        back = back[:size] + back[size : 2 * size] + back[2 * size :]
        for i, k in enumerate(used):
            surf[k, j] = back[i * XT : (i + 1) * XT]


def forward_kernel(
    source_pos, source_wave, u0, u1, s, even, odd, other, receivers, observed, l6, l7,
    w1, w2, w3, w4, w5, d1, d2, d3, d4, d5, diag, cx, cy, cz, surf, m6, m5, m4, m3, m_before, g6, g5, g4,
    stiff, before, edge,
):
    lane, tile = iotas()
    waves = (w1, w2, w3, w4, w5)
    slopes = (d1, d2, d3, d4)
    for ext, own in ((stiff, s), (w1, u1), (before, u0)):
        fill(ext, own, OFF)
    core = core_index()

    def halos(low, high):
        for part, base in ((0, core * PART), (1, (1 - core) * PART)):
            for k in range(REACH):
                stiff[OFF - REACH + k, pl.ds(base, PART)] = low[part][k * PART : (k + 1) * PART]
                stiff[OFF + ROWS + k, pl.ds(base, PART)] = high[part][k * PART : (k + 1) * PART]
        low, high = low[0], high[0]
        fill_cone(stiff, low, high, REACH * PART, REACH)
        at = TILE_S
        fill_halo(w1, OFF, low, high, at, REACH)
        at += REACH * NZ
        fill_halo(before, OFF, low, high, at, REACH - 1)
        at += (REACH - 1) * NZ
        fill_cone(w1, low, high, at, REACH)
        fill_cone(before, low, high, at + TIP, REACH - 1)
        for i, ref in enumerate((low, high)):
            edge[2 * i] = ref[TILE_A - 2]
            edge[2 * i + 1] = ref[TILE_A - 1]

    by_parity(((even, other.at[:TILE_S]), (odd, other.at[TILE_S:])), halos)
    coefficients(stiff, diag, cx, cy, cz, lane, tile)
    gy = lax.axis_index("gy")

    @pl.when(gy == 0)
    def _():
        cy[OFF - 1] = jnp.zeros((NZ, XT, LANES), f32)

    @pl.when(gy == lax.axis_size("gy") - 1)
    def _():
        cy[OFF + ROWS - 1] = jnp.zeros((NZ, XT, LANES), f32)

    z_src = source_pos[0, 0]
    e_src = source_pos[0, 1] - gy * ROWS + OFF
    x_src = source_pos[0, 2]
    spot = (tile * LANES + lane) == x_src
    for k in range(STEPS):
        older = before if k == 0 else waves[k - 1]
        after = waves[k + 1]
        leap(waves[k], older, after, 0, diag, cx, cy, cz, step_rows(k, True), lane, slopes[k])
        reach = STEPS - k + CONE

        @pl.when((e_src >= OFF - reach) & (e_src < OFF + ROWS + reach))
        def _():
            add = jnp.where(spot, TIME_STEP_SQ * source_wave[0, k], 0.0)
            after[e_src, z_src] = after[e_src, z_src] + add

    def last_slope(i, carry):
        for y in (4 * i + r for r in range(4)):
            for z in range(NZ):
                u = w5[OFF + y, z]
                d5[y, z] = x_next(u, lane) - u
        return carry

    lax.fori_loop(0, ROWS // 4, last_slope, 0)
    edges = [jnp.concatenate([edge[2 * i], edge[2 * i + 1]], 0) for i in range(2)]
    misfit_surfaces(waves, receivers, observed, edges, surf, lane, tile)

    fill(m6, l6, REACH)
    fill(m_before, l7, REACH)
    lams = (m6, m5, m4, m3)
    for k, slope in enumerate((g6, g5, g4)):
        older = m_before if k == 0 else lams[k - 1]
        leap(
            lams[k], older, lams[k + 1], OFF - REACH, diag, cx, cy, cz, inner_rows(k), lane, slope, surf.at[STEPS - 1 - k]
        )


def forward(*args):
    one = jax.ShapeDtypeStruct(FIELD, f32)
    own = jax.ShapeDtypeStruct((ROWS, NZ, XT, LANES), f32)
    surf = jax.ShapeDtypeStruct((STEPS, SURF_ROWS, XT, LANES), f32)
    short = jax.ShapeDtypeStruct(SHORT, f32)
    outs = (one,) * (STEPS + 1) + (own,) * (STEPS + 1) + (one,) * 4 + (surf,) + (short,) * 5 + (own,) * 3
    return pl.pallas_call(
        forward_kernel,
        out_shape=outs,
        in_specs=[SMEM] * 2 + [VMEM] * (len(args) - 2),
        out_specs=(VMEM,) * len(outs),
        scratch_shapes=[pltpu.VMEM(FIELD, f32)] * 2 + [pltpu.VMEM((4, XT, LANES), f32)],
        compiler_params=pltpu.CompilerParams(vmem_limit_bytes=16 << 20),
        cost_estimate=pl.CostEstimate(flops=1 << 25, bytes_accessed=1 << 24, transcendentals=0),
        name="forward",
    )(*args)


def adjoint_kernel(
    odd, even, w1, w2, w3, w4, w5, d1, d2, d3, d4, d5, diag, cx, cy, cz, surf, *rest
):
    m6, m5, m4, m3, before, g6, g5, g4, keep, send, m2, g3, face_y, grad = rest[8:]
    lane, tile = iotas()
    x_end = (lane == LANES - 1) & (tile == XT - 1)
    x_side = x_end | ((lane == 0) & (tile == 0))
    lams = (m6, m5, m4, m3, m2)
    slopes = (g6, g5, g4, g3)

    def halos(low, high):
        fill_halo(m6, REACH, low, high, 0, REACH)
        fill_halo(before, REACH, low, high, REACH * NZ, REACH - 1)

    by_parity((even, odd), halos)
    for k in range(STEPS):
        older = before if k == 0 else lams[k - 1]
        rows = step_rows(k, False, inner_rows(k))
        leap(lams[k], older, lams[k + 1], OFF - REACH, diag, cx, cy, cz, rows, lane, slopes[k], surf.at[STEPS - 1 - k])

    pairs = ((w5, m6, d5, g6), (w4, m5, d4, g5), (w3, m4, d3, g4), (w2, m3, d2, g3), (w1, m2, d1, None))
    for z in range(NZ):
        total = None
        for w, m, _, _ in pairs:
            part = (w[OFF, z] - w[OFF - 1, z]) * (m[REACH, z] - m[REACH - 1, z])
            total = part if total is None else total + part
        face_y[z] = total

    def two_rows(i, carry):
        below_y = [face_y[z] for z in range(NZ)]
        for y in (2 * i, 2 * i + 1):
            e = y + OFF
            below = None
            us = [w[e, 0] for w, _, _, _ in pairs]
            f = y + REACH
            ls = [m[f, 0] for _, m, _, _ in pairs]
            for z in range(NZ):
                fx = fy = fz = cell = None
                next_us, next_ls = [], []
                for (w, m, d, g), u, l in zip(pairs, us, ls, strict=True):
                    px = d[y, z] * (g[y, z] if g is not None else x_next(l, lane) - l)
                    py = (w[e + 1, z] - u) * (m[f + 1, z] - l)
                    both = u * l
                    if z < NZ - 1:
                        un, ln = w[e, z + 1], m[f, z + 1]
                        next_us.append(un)
                        next_ls.append(ln)
                        pz = (un - u) * (ln - l)
                    else:
                        pz = both
                    fx = px if fx is None else fx + px
                    fy = py if fy is None else fy + py
                    fz = pz if fz is None else fz + pz
                    cell = both if cell is None else cell + both
                us, ls = next_us, next_ls
                fx = jnp.where(x_end, 0.0, fx)
                total = fx + x_prev(fx, lane) + jnp.where(x_side, cell, 0.0)
                total = total + fy + below_y[z] + fz + (cell if z == 0 else below)
                below_y[z] = fy
                below = fz
                grad[z, pl.ds(y, XT, stride=ROWS), :] = -HALF * total
        for z in range(NZ):
            face_y[z] = below_y[z]
        return carry

    lax.fori_loop(0, ROWS // 2, two_rows, 0)
    core = core_index()
    for group in range(2):
        keep[group] = grad[pl.ds(8 * group + 4 * core, 4)]
        send[group] = grad[pl.ds(8 * group + 4 * (1 - core), 4)]


def adjoint(*args):
    part = jax.ShapeDtypeStruct((2, 4, XT * ROWS, LANES), f32)
    own = jax.ShapeDtypeStruct((ROWS, NZ, XT, LANES), f32)
    outs = (jax.ShapeDtypeStruct(SHORT, f32),) * 5 + (own,) * 3 + (part, part)
    first = len(args) - 8
    return pl.pallas_call(
        adjoint_kernel,
        out_shape=outs,
        in_specs=[VMEM] * len(args),
        out_specs=(VMEM,) * len(outs),
        input_output_aliases={first + i: i for i in range(8)},
        scratch_shapes=[
            pltpu.VMEM(SHORT, f32),
            pltpu.VMEM((ROWS, NZ, XT, LANES), f32),
            pltpu.VMEM((NZ, XT, LANES), f32),
            pltpu.VMEM((NZ, XT * ROWS, LANES), f32),
        ],
        compiler_params=pltpu.CompilerParams(vmem_limit_bytes=16 << 20),
        cost_estimate=pl.CostEstimate(flops=1 << 25, bytes_accessed=1 << 24, transcendentals=0),
        name="adjoint",
    )(*args)[-2:]


def finish_kernel(mine, other, out, sems):
    core = core_index()
    copies = []
    for group in range(2):
        for i, (part, base) in enumerate(((mine, core), (other, 1 - core))):
            target = out.at[pl.ds(8 * group + 4 * base, 4)]
            copies.append(pltpu.make_async_copy(part.at[group], target, sems.at[2 * group + i]))
    for copy in copies:
        copy.start()
    for copy in copies:
        copy.wait()


def finish(mine, other):
    return pl.pallas_call(
        finish_kernel,
        out_shape=jax.ShapeDtypeStruct((NZ, XT * ROWS, LANES), f32),
        in_specs=[VMEM, VMEM],
        out_specs=pl.BlockSpec(memory_space=pl.ANY),
        scratch_shapes=[pltpu.SemaphoreType.DMA((4,))],
        compiler_params=pltpu.CompilerParams(vmem_limit_bytes=2 << 20),
        name="finish",
    )(mine, other)


def swap_even(block):
    count = lax.axis_size("gy")
    pairs = [(i, i + 1) for i in range(0, count - 1, 2)]
    return lax.ppermute(block, "gy", pairs + [(j, i) for i, j in pairs])


def swap_odd(block):
    count = lax.axis_size("gy")
    pairs = [(i, i + 1) for i in range(1, count - 1, 2)]
    return lax.ppermute(block, "gy", pairs + [(j, i) for i, j in pairs])


def swap_core(block):
    return lax.ppermute(block, "shot", [(0, 1), (1, 0), (2, 3), (3, 2)])


def swap_far(block):
    return lax.ppermute(block, "shot", [(0, 2), (2, 0), (1, 3), (3, 1)])


def body(
    stiffness,
    first_moment,
    second_moment,
    wave_prev,
    wave_now,
    adjoint_next,
    adjoint_now,
    observed,
    receiver_x,
    source_pos,
    source_wave,
):
    shot = lax.axis_index("shot")
    core, far = shot % 2, shot // 2
    s = native(stiffness)
    u0, u1 = native(wave_prev[0]), native(wave_now[0])
    l6, l7 = native(adjoint_now[0]), native(adjoint_next[0])
    first, second = native(first_moment), native(second_moment)

    a_even, a_odd = pack(pack_first_kernel, "pack_first", TILE_A, s, u1, u0, receiver_x[0], observed[0])
    l_even, l_odd = pack(pack_adjoint_kernel, "pack_adjoint", TILE_L, l6, l7)
    a_even, a_odd = swap_even(a_even), swap_odd(a_odd)
    moments = jnp.stack([first, second])
    l_even, l_odd, moments, a_even = lax.optimization_barrier((l_even, l_odd, moments, a_even))
    l_even, l_odd, moments = swap_even(l_even), swap_odd(l_odd), swap_far(moments)
    other = swap_core(jnp.concatenate([a_even[:TILE_S], a_odd[:TILE_S]]))
    fields = forward(
        source_pos, source_wave, u0, u1, s, a_even, a_odd, other, receiver_x[0], observed[0], l6, l7
    )
    keep, send = adjoint(l_odd, l_even, *fields)
    keep, send, moments = lax.optimization_barrier((keep, send, moments))
    chip_sum = keep + swap_core(send)
    share = chip_sum + swap_far(chip_sum)
    first_two = jnp.where(far == 0, jnp.stack([first, moments[0]]), jnp.stack([moments[0], first]))
    second_two = jnp.where(far == 0, jnp.stack([second, moments[1]]), jnp.stack([moments[1], second]))
    halves = s.reshape(2, 2, 4, XT * ROWS, LANES)
    stiff_two = jnp.where(core == 0, halves[:, 0], halves[:, 1])
    first_new = BETA_ONE * first_two + (1.0 - BETA_ONE) * share
    second_new = BETA_TWO * second_two + (1.0 - BETA_TWO) * share * share
    updated = stiff_two - LEARN_RATE * (first_new / (1.0 - BETA_ONE**ADAM_TICKS)) / (
        jnp.sqrt(second_new / (1.0 - BETA_TWO**ADAM_TICKS)) + ADAM_EPS
    )
    stiffness_new = finish(updated, swap_core(updated))
    first_new = jnp.where(far == 0, first_new[0], first_new[1])
    second_new = jnp.where(far == 0, second_new[0], second_new[1])
    return (from_native(stiffness_new), from_native(first_new), from_native(second_new))


def solution(mesh):
    return jax.shard_map(
        body,
        mesh=mesh,
        in_specs=(
            P(None, "gy", None),
            P("shot", "gy", None),
            P("shot", "gy", None),
            P("shot", None, "gy", None),
            P("shot", None, "gy", None),
            P("shot", None, "gy", None),
            P("shot", None, "gy", None),
            P("shot", None, "gy", None),
            P("shot", "gy", None),
            P("shot", None),
            P("shot", None),
        ),
        out_specs=(P(None, "gy", None), P("shot", "gy", None), P("shot", "gy", None)),
        check_vma=False,
    )
```

```python
import functools

import jax
import jax.numpy as jnp
from jax import lax
from jax.experimental import pallas as pl
from jax.experimental.pallas import tpu as pltpu
from jax.sharding import PartitionSpec as P

TIME_STEP_SQ = 0.15
BETA_ONE = 0.9
BETA_TWO = 0.999
LEARN_RATE = 0.05
ADAM_EPS = 1e-08
ADAM_TICKS = 10.0

NZ = 16
ROWS = 8
XT = 8
LANES = 128
STEPS = 4
REACH = STEPS + 1
EDGE = STEPS
CONE = STEPS - 1
OFF = ROWS
EXT = ROWS + 2 * OFF
FIELD = (EXT, NZ, XT, LANES)
SHORT = (ROWS + 2 * REACH, NZ, XT, LANES)
SURF_ROWS = ROWS + 2 * EDGE
PART = NZ // 2
TIP = CONE * (CONE + 1) // 2
TILE_S = REACH * PART + TIP
TILE_U = (2 * REACH - 1) * NZ + 2 * TIP + 2
TILE_A = TILE_S + TILE_U
TILE_L = (2 * REACH - 1) * NZ
HALF = 0.5 * TIME_STEP_SQ
PACK_VMEM = 56 << 20

f32 = jnp.float32
VMEM = pl.BlockSpec(memory_space=pltpu.VMEM)
SMEM = pl.BlockSpec(memory_space=pltpu.SMEM)


def native(block):
    planes = block.shape[0]
    return block.reshape(planes, ROWS, XT, LANES).transpose(0, 2, 1, 3).reshape(planes, XT * ROWS, LANES)


def from_native(block):
    planes = block.shape[0]
    return block.reshape(planes, XT, ROWS, LANES).transpose(0, 2, 1, 3).reshape(planes, ROWS, XT * LANES)


def row_of(ref, z, y):
    return ref[z, pl.ds(y, XT, stride=ROWS), :]


def x_next(f, lane):
    r = pltpu.roll(f, LANES - 1, 1)
    return jnp.where(lane == LANES - 1, pltpu.roll(r, XT - 1, 0), r)


def x_prev(f, lane):
    r = pltpu.roll(f, 1, 1)
    return jnp.where(lane == 0, pltpu.roll(r, 1, 0), r)


def iotas():
    lane = lax.broadcasted_iota(jnp.int32, (XT, LANES), 1)
    tile = lax.broadcasted_iota(jnp.int32, (XT, LANES), 0)
    return lane, tile


def in_blocks(lo, hi, size, rows):
    whole = (hi - lo) // size
    if whole:
        lax.fori_loop(0, whole, lambda i, c: (rows(lo + i * size, size), c)[1], 0)
    if (hi - lo) % size:
        rows(lo + whole * size, (hi - lo) % size)


def pack_fields(fields, widths, low, high, at):
    def plane(z, carry):
        first = at
        for ref, width in zip(fields, widths, strict=True):
            for k in range(width):
                low[first + k * NZ + z] = row_of(ref, z, k)
                high[first + k * NZ + z] = row_of(ref, z, ROWS - width + k)
            first += width * NZ
        return carry

    lax.fori_loop(0, NZ, plane, 0)
    return at + sum(widths) * NZ


def core_index():
    return lax.rem(lax.axis_index("shot"), 2)


def by_parity(pair, work):
    parity = lax.rem(lax.axis_index("gy"), 2)

    @pl.when(parity == 0)
    def _():
        work(pair[1], pair[0])

    @pl.when(parity == 1)
    def _():
        work(pair[0], pair[1])


def pack_cone(ref, width, low, high, at):
    for k in range(CONE):
        for z in range(CONE - k):
            low[at] = row_of(ref, z, width + k)
            high[at] = row_of(ref, z, ROWS - 1 - width - k)
            at += 1
    return at


def fetch(sources, places, sems):
    copies = [pltpu.make_async_copy(a, b, sems.at[i]) for i, (a, b) in enumerate(zip(sources, places, strict=True))]
    for copy in copies:
        copy.start()
    for copy in copies:
        copy.wait()


def pack_first_kernel(
    s_far, u1_far, u0_far, receivers_far, observed_far, even, odd, s, u1, u0, receivers, observed, sems
):
    fetch((s_far, u1_far, u0_far, receivers_far, observed_far), (s, u1, u0, receivers, observed), sems)
    base = core_index() * PART

    def work(low, high):
        def plane(z, carry):
            for k in range(REACH):
                low[k * PART + z] = row_of(s, base + z, k)
                high[k * PART + z] = row_of(s, base + z, ROWS - REACH + k)
            return carry

        lax.fori_loop(0, PART, plane, 0)
        at = pack_cone(s, REACH, low, high, REACH * PART)
        at = pack_fields((u1, u0), (REACH, REACH - 1), low, high, at)
        at = pack_cone(u1, REACH, low, high, at)
        at = pack_cone(u0, REACH - 1, low, high, at)
        where = receivers[...].astype(f32)
        empty = jnp.zeros((2, LANES), f32)
        for side, rows in ((low, lambda n: slice(0, n)), (high, lambda n: slice(ROWS - n, ROWS))):
            parts = [where[rows(EDGE)]]
            for k in range(STEPS - 1, -1, -1):
                parts.append(observed[k][rows(k + 1)])
            parts.append(empty)
            both = jnp.concatenate(parts, 0)
            side[at] = both[:XT]
            side[at + 1] = both[XT:]

    by_parity((even, odd), work)


def pack_adjoint_kernel(l6_far, l7_far, even, odd, l6, l7, sems):
    fetch((l6_far, l7_far), (l6, l7), sems)
    by_parity((even, odd), lambda low, high: pack_fields((l6, l7), (REACH, REACH - 1), low, high, 0))


def pack(kernel, name, tiles, *arrays):
    shape = pltpu.VMEM((tiles, XT, LANES), f32)
    return pl.pallas_call(
        kernel,
        out_shape=(shape, shape),
        in_specs=[pl.BlockSpec(memory_space=pl.ANY)] * len(arrays),
        out_specs=(VMEM, VMEM),
        scratch_shapes=[pltpu.VMEM(a.shape, a.dtype) for a in arrays] + [pltpu.SemaphoreType.DMA((len(arrays),))],
        compiler_params=pltpu.CompilerParams(vmem_limit_bytes=PACK_VMEM),
        cost_estimate=pl.CostEstimate(flops=0, bytes_accessed=1 << 16, transcendentals=0),
        name=name,
    )(*arrays)


def fill(ext, own, off):
    def plane(z, carry):
        for k in range(ROWS):
            ext[off + k, z] = row_of(own, z, k)
        return carry

    lax.fori_loop(0, NZ, plane, 0)


def fill_halo(ext, off, low, high, at, width):
    for k in range(width):
        ext[off - width + k] = low[at + k * NZ : at + (k + 1) * NZ]
        ext[off + ROWS + k] = high[at + k * NZ : at + (k + 1) * NZ]


def fill_cone(ext, low, high, at, width):
    for k in range(CONE):
        planes = CONE - k
        ext[OFF - 1 - width - k, :planes] = low[at : at + planes]
        ext[OFF + ROWS + width + k, :planes] = high[at : at + planes]
        at += planes


def coefficients(stiff, diag, cx, cy, cz, lane, tile):
    x_end = (lane == LANES - 1) & (tile == XT - 1)
    x_start = (lane == 0) & (tile == 0)
    top, bottom = OFF - REACH, OFF + ROWS + REACH

    def face_y(e, planes):
        for z in range(planes):
            cy[e, z] = HALF * (stiff[e, z] + stiff[e + 1, z])

    def cells(e, planes):
        below = None
        following = HALF * stiff[e, 0]
        for z in range(planes):
            s = following
            face = s + jnp.where(x_end, 0.0, x_next(s, lane))
            total = face + (s + jnp.where(x_start, 0.0, x_prev(s, lane)))
            if z < NZ - 1:
                following = HALF * stiff[e, z + 1]
                above = s + following
            else:
                above = s
            total = total + above + (below if z > 0 else s) + cy[e, z] + cy[e - 1, z]
            cx[e, z] = jnp.where(x_end, 0.0, face)
            cz[e, z] = above
            diag[e, z] = 2.0 - total
            below = above

    def faces(first, count):
        for r in range(count):
            face_y(first + r, NZ)

    def rows(first, count):
        for r in range(count):
            cells(first + r, NZ)

    in_blocks(top, bottom - 1, 4, faces)
    for k in range(CONE):
        face_y(top - 1 - k, CONE - k)
        face_y(bottom - 1 + k, CONE - k)
    in_blocks(top + 1, bottom - 1, 4, rows)
    for k in range(CONE):
        cells(top - k, CONE - k)
        cells(bottom - 1 + k, CONE - k)


def leap(now, before, after, base, diag, cx, cy, cz, rows, lane, slope, inject=None):
    for e, planes in rows:
        f = e - base
        for z in range(planes):
            u = now[f, z]
            c = cx[e, z]
            following = x_next(u, lane)
            acc = diag[e, z] * u - before[f, z]
            acc = acc + c * following + x_prev(c * u, lane)
            acc = acc + cy[e, z] * now[f + 1, z] + cy[e - 1, z] * now[f - 1, z]
            if z < NZ - 1:
                acc = acc + cz[e, z] * now[f, z + 1]
            if z > 0:
                acc = acc + cz[e, z - 1] * now[f, z - 1]
            if z == 0 and inject is not None:
                acc = acc + inject[e - OFF + EDGE]
            after[f, z] = acc
            if OFF <= e < OFF + ROWS:
                slope[e - OFF, z] = following - u


def inner_rows(k):
    return [(OFF + y, NZ) for y in range(k + 1, ROWS - 1 - k)]


def step_rows(k, cone, skip=()):
    whole = STEPS - k
    rows = [(OFF + y, NZ) for y in range(ROWS)]
    rows += [(OFF - whole + j, NZ) for j in range(whole)] + [(OFF + ROWS + j, NZ) for j in range(whole)]
    if cone:
        for j in range(CONE):
            planes = min(CONE - j, whole)
            rows += [(OFF - 1 - whole - j, planes), (OFF + ROWS + whole + j, planes)]
    return [row for row in rows if row not in skip]


def three_parts(f):
    parts = []
    for _ in range(3):
        part = f.astype(jnp.bfloat16)
        parts.append(part.astype(f32))
        f = f - parts[-1]
    return jnp.concatenate(parts, 0).astype(jnp.bfloat16)


def misfit_surfaces(waves, receivers, observed, edges, surf, lane, tile):
    column = lax.broadcasted_iota(jnp.int32, (LANES, LANES), 0)
    plan = []
    for j in range(SURF_ROWS):
        y = j - EDGE
        if y < 0:
            used, at = range(-y - 1, STEPS), edges[0][:EDGE].astype(jnp.int32)[j : j + 1]
        elif y < ROWS:
            used, at = range(STEPS), receivers[y : y + 1, :]
        else:
            used, at = range(y - ROWS, STEPS), edges[1][:EDGE].astype(jnp.int32)[y - ROWS : y - ROWS + 1]
        pick = jnp.where(column == (at & (LANES - 1)), 1.0, 0.0).astype(jnp.bfloat16)
        held = jnp.where(tile == (at >> 7), 1.0, 0.0)
        surface = jnp.concatenate([waves[k + 1][OFF + y, 0] for k in used], 0)
        lanes_of = jnp.dot(three_parts(surface), pick, preferred_element_type=f32)
        plan.append((j, used, pick, held, lanes_of))
    for j, used, pick, held, lanes_of in plan:
        y = j - EDGE
        size = len(used) * XT
        lanes_of = lanes_of[:size] + lanes_of[size : 2 * size] + lanes_of[2 * size :]
        parts = []
        for i, k in enumerate(used):
            record = jnp.sum(lanes_of[i * XT : (i + 1) * XT] * held, axis=0, keepdims=True)
            if 0 <= y < ROWS:
                trace = observed[k, y : y + 1, :]
            else:
                skip = EDGE + sum(m + 1 for m in range(k + 1, STEPS))
                r = skip + (y + k + 1 if y < 0 else y - ROWS)
                trace = edges[0 if y < 0 else 1][r : r + 1]
            parts.append(held * (record - trace))
        back = lax.dot_general(
            three_parts(jnp.concatenate(parts, 0)), pick, (((1,), (1,)), ((), ())), preferred_element_type=f32
        )
        back = back[:size] + back[size : 2 * size] + back[2 * size :]
        for i, k in enumerate(used):
            surf[k, j] = back[i * XT : (i + 1) * XT]


def forward_kernel(
    source_pos, source_wave, u0, u1, s, even, odd, other, receivers, observed, l6, l7,
    w1, w2, w3, w4, w5, d1, d2, d3, d4, d5, diag, cx, cy, cz, surf, m6, m5, m4, m3, m_before, g6, g5, g4,
    stiff, before, edge,
):
    lane, tile = iotas()
    waves = (w1, w2, w3, w4, w5)
    slopes = (d1, d2, d3, d4)
    for ext, own in ((stiff, s), (w1, u1), (before, u0)):
        fill(ext, own, OFF)
    core = core_index()

    def halos(low, high):
        for part, base in ((0, core * PART), (1, (1 - core) * PART)):
            for k in range(REACH):
                stiff[OFF - REACH + k, pl.ds(base, PART)] = low[part][k * PART : (k + 1) * PART]
                stiff[OFF + ROWS + k, pl.ds(base, PART)] = high[part][k * PART : (k + 1) * PART]
        low, high = low[0], high[0]
        fill_cone(stiff, low, high, REACH * PART, REACH)
        at = TILE_S
        fill_halo(w1, OFF, low, high, at, REACH)
        at += REACH * NZ
        fill_halo(before, OFF, low, high, at, REACH - 1)
        at += (REACH - 1) * NZ
        fill_cone(w1, low, high, at, REACH)
        fill_cone(before, low, high, at + TIP, REACH - 1)
        for i, ref in enumerate((low, high)):
            edge[2 * i] = ref[TILE_A - 2]
            edge[2 * i + 1] = ref[TILE_A - 1]

    by_parity(((even, other.at[:TILE_S]), (odd, other.at[TILE_S:])), halos)
    coefficients(stiff, diag, cx, cy, cz, lane, tile)
    gy = lax.axis_index("gy")

    @pl.when(gy == 0)
    def _():
        cy[OFF - 1] = jnp.zeros((NZ, XT, LANES), f32)

    @pl.when(gy == lax.axis_size("gy") - 1)
    def _():
        cy[OFF + ROWS - 1] = jnp.zeros((NZ, XT, LANES), f32)

    z_src = source_pos[0, 0]
    e_src = source_pos[0, 1] - gy * ROWS + OFF
    x_src = source_pos[0, 2]
    spot = (tile * LANES + lane) == x_src
    for k in range(STEPS):
        older = before if k == 0 else waves[k - 1]
        after = waves[k + 1]
        leap(waves[k], older, after, 0, diag, cx, cy, cz, step_rows(k, True), lane, slopes[k])
        reach = STEPS - k + CONE

        @pl.when((e_src >= OFF - reach) & (e_src < OFF + ROWS + reach))
        def _():
            add = jnp.where(spot, TIME_STEP_SQ * source_wave[0, k], 0.0)
            after[e_src, z_src] = after[e_src, z_src] + add

    def last_slope(i, carry):
        for y in (4 * i + r for r in range(4)):
            for z in range(NZ):
                u = w5[OFF + y, z]
                d5[y, z] = x_next(u, lane) - u
        return carry

    lax.fori_loop(0, ROWS // 4, last_slope, 0)
    edges = [jnp.concatenate([edge[2 * i], edge[2 * i + 1]], 0) for i in range(2)]
    misfit_surfaces(waves, receivers, observed, edges, surf, lane, tile)

    fill(m6, l6, REACH)
    fill(m_before, l7, REACH)
    lams = (m6, m5, m4, m3)
    for k, slope in enumerate((g6, g5, g4)):
        older = m_before if k == 0 else lams[k - 1]
        leap(
            lams[k], older, lams[k + 1], OFF - REACH, diag, cx, cy, cz, inner_rows(k), lane, slope, surf.at[STEPS - 1 - k]
        )


def forward(*args):
    one = jax.ShapeDtypeStruct(FIELD, f32)
    own = jax.ShapeDtypeStruct((ROWS, NZ, XT, LANES), f32)
    surf = jax.ShapeDtypeStruct((STEPS, SURF_ROWS, XT, LANES), f32)
    short = jax.ShapeDtypeStruct(SHORT, f32)
    outs = (one,) * (STEPS + 1) + (own,) * (STEPS + 1) + (one,) * 4 + (surf,) + (short,) * 5 + (own,) * 3
    return pl.pallas_call(
        forward_kernel,
        out_shape=outs,
        in_specs=[SMEM] * 2 + [VMEM] * (len(args) - 2),
        out_specs=(VMEM,) * len(outs),
        scratch_shapes=[pltpu.VMEM(FIELD, f32)] * 2 + [pltpu.VMEM((4, XT, LANES), f32)],
        compiler_params=pltpu.CompilerParams(vmem_limit_bytes=16 << 20),
        cost_estimate=pl.CostEstimate(flops=1 << 25, bytes_accessed=1 << 24, transcendentals=0),
        name="forward",
    )(*args)


def adjoint_kernel(
    odd, even, w1, w2, w3, w4, w5, d1, d2, d3, d4, d5, diag, cx, cy, cz, surf, *rest
):
    m6, m5, m4, m3, before, g6, g5, g4, keep, send, m2, g3, face_y, grad = rest[8:]
    lane, tile = iotas()
    x_end = (lane == LANES - 1) & (tile == XT - 1)
    x_side = x_end | ((lane == 0) & (tile == 0))
    lams = (m6, m5, m4, m3, m2)
    slopes = (g6, g5, g4, g3)

    def halos(low, high):
        fill_halo(m6, REACH, low, high, 0, REACH)
        fill_halo(before, REACH, low, high, REACH * NZ, REACH - 1)

    by_parity((even, odd), halos)
    for k in range(STEPS):
        older = before if k == 0 else lams[k - 1]
        rows = step_rows(k, False, inner_rows(k))
        leap(lams[k], older, lams[k + 1], OFF - REACH, diag, cx, cy, cz, rows, lane, slopes[k], surf.at[STEPS - 1 - k])

    pairs = ((w5, m6, d5, g6), (w4, m5, d4, g5), (w3, m4, d3, g4), (w2, m3, d2, g3), (w1, m2, d1, None))
    for z in range(NZ):
        total = None
        for w, m, _, _ in pairs:
            part = (w[OFF, z] - w[OFF - 1, z]) * (m[REACH, z] - m[REACH - 1, z])
            total = part if total is None else total + part
        face_y[z] = total

    def two_rows(i, carry):
        below_y = [face_y[z] for z in range(NZ)]
        for y in (2 * i, 2 * i + 1):
            e = y + OFF
            below = None
            us = [w[e, 0] for w, _, _, _ in pairs]
            f = y + REACH
            ls = [m[f, 0] for _, m, _, _ in pairs]
            for z in range(NZ):
                fx = fy = fz = cell = None
                next_us, next_ls = [], []
                for (w, m, d, g), u, l in zip(pairs, us, ls, strict=True):
                    px = d[y, z] * (g[y, z] if g is not None else x_next(l, lane) - l)
                    py = (w[e + 1, z] - u) * (m[f + 1, z] - l)
                    both = u * l
                    if z < NZ - 1:
                        un, ln = w[e, z + 1], m[f, z + 1]
                        next_us.append(un)
                        next_ls.append(ln)
                        pz = (un - u) * (ln - l)
                    else:
                        pz = both
                    fx = px if fx is None else fx + px
                    fy = py if fy is None else fy + py
                    fz = pz if fz is None else fz + pz
                    cell = both if cell is None else cell + both
                us, ls = next_us, next_ls
                fx = jnp.where(x_end, 0.0, fx)
                total = fx + x_prev(fx, lane) + jnp.where(x_side, cell, 0.0)
                total = total + fy + below_y[z] + fz + (cell if z == 0 else below)
                below_y[z] = fy
                below = fz
                grad[z, pl.ds(y, XT, stride=ROWS), :] = -HALF * total
        for z in range(NZ):
            face_y[z] = below_y[z]
        return carry

    lax.fori_loop(0, ROWS // 2, two_rows, 0)
    core = core_index()
    for group in range(2):
        keep[group] = grad[pl.ds(8 * group + 4 * core, 4)]
        send[group] = grad[pl.ds(8 * group + 4 * (1 - core), 4)]


def adjoint(*args):
    part = jax.ShapeDtypeStruct((2, 4, XT * ROWS, LANES), f32)
    own = jax.ShapeDtypeStruct((ROWS, NZ, XT, LANES), f32)
    outs = (jax.ShapeDtypeStruct(SHORT, f32),) * 5 + (own,) * 3 + (part, part)
    first = len(args) - 8
    return pl.pallas_call(
        adjoint_kernel,
        out_shape=outs,
        in_specs=[VMEM] * len(args),
        out_specs=(VMEM,) * len(outs),
        input_output_aliases={first + i: i for i in range(8)},
        scratch_shapes=[
            pltpu.VMEM(SHORT, f32),
            pltpu.VMEM((ROWS, NZ, XT, LANES), f32),
            pltpu.VMEM((NZ, XT, LANES), f32),
            pltpu.VMEM((NZ, XT * ROWS, LANES), f32),
        ],
        compiler_params=pltpu.CompilerParams(vmem_limit_bytes=16 << 20),
        cost_estimate=pl.CostEstimate(flops=1 << 25, bytes_accessed=1 << 24, transcendentals=0),
        name="adjoint",
    )(*args)[-2:]


def blend_kernel(first, second, moments, first_two, second_two):
    far = lax.axis_index("shot") // 2
    first_two[far] = BETA_ONE * first[...]
    first_two[1 - far] = BETA_ONE * moments[0]
    second_two[far] = BETA_TWO * second[...]
    second_two[1 - far] = BETA_TWO * moments[1]


def blend(first, second, moments):
    two = jax.ShapeDtypeStruct((2, 4, XT * ROWS, LANES), f32)
    return pl.pallas_call(
        blend_kernel,
        out_shape=(two, two),
        in_specs=[VMEM] * 3,
        out_specs=(VMEM, VMEM),
        compiler_params=pltpu.CompilerParams(vmem_limit_bytes=4 << 20),
        cost_estimate=pl.CostEstimate(flops=0, bytes_accessed=1 << 24, transcendentals=0),
        name="blend",
    )(first, second, moments)


def finish_kernel(mine, other, out, sems):
    core = core_index()
    copies = []
    for group in range(2):
        for i, (part, base) in enumerate(((mine, core), (other, 1 - core))):
            target = out.at[pl.ds(8 * group + 4 * base, 4)]
            copies.append(pltpu.make_async_copy(part.at[group], target, sems.at[2 * group + i]))
    for copy in copies:
        copy.start()
    for copy in copies:
        copy.wait()


def finish(mine, other):
    return pl.pallas_call(
        finish_kernel,
        out_shape=jax.ShapeDtypeStruct((NZ, XT * ROWS, LANES), f32),
        in_specs=[VMEM, VMEM],
        out_specs=pl.BlockSpec(memory_space=pl.ANY),
        scratch_shapes=[pltpu.SemaphoreType.DMA((4,))],
        compiler_params=pltpu.CompilerParams(vmem_limit_bytes=2 << 20),
        name="finish",
    )(mine, other)


def swap_even(block):
    count = lax.axis_size("gy")
    pairs = [(i, i + 1) for i in range(0, count - 1, 2)]
    return lax.ppermute(block, "gy", pairs + [(j, i) for i, j in pairs])


def swap_odd(block):
    count = lax.axis_size("gy")
    pairs = [(i, i + 1) for i in range(1, count - 1, 2)]
    return lax.ppermute(block, "gy", pairs + [(j, i) for i, j in pairs])


def swap_core(block):
    return lax.ppermute(block, "shot", [(0, 1), (1, 0), (2, 3), (3, 2)])


def swap_far(block):
    return lax.ppermute(block, "shot", [(0, 2), (2, 0), (1, 3), (3, 1)])


def body(
    stiffness,
    first_moment,
    second_moment,
    wave_prev,
    wave_now,
    adjoint_next,
    adjoint_now,
    observed,
    receiver_x,
    source_pos,
    source_wave,
):
    shot = lax.axis_index("shot")
    core, far = shot % 2, shot // 2
    s = native(stiffness)
    u0, u1 = native(wave_prev[0]), native(wave_now[0])
    l6, l7 = native(adjoint_now[0]), native(adjoint_next[0])
    first, second = native(first_moment), native(second_moment)

    a_even, a_odd = pack(pack_first_kernel, "pack_first", TILE_A, s, u1, u0, receiver_x[0], observed[0])
    l_even, l_odd = pack(pack_adjoint_kernel, "pack_adjoint", TILE_L, l6, l7)
    a_even, a_odd = swap_even(a_even), swap_odd(a_odd)
    moments = jnp.stack([first, second])
    l_even, l_odd, moments, a_even = lax.optimization_barrier((l_even, l_odd, moments, a_even))
    l_even, l_odd, moments = swap_even(l_even), swap_odd(l_odd), swap_far(moments)
    other = swap_core(jnp.concatenate([a_even[:TILE_S], a_odd[:TILE_S]]))
    fields = forward(
        source_pos, source_wave, u0, u1, s, a_even, a_odd, other, receiver_x[0], observed[0], l6, l7
    )
    keep, send = adjoint(l_odd, l_even, *fields)
    keep, moments = lax.optimization_barrier((keep, moments))
    first_two, second_two = blend(first, second, moments)
    chip_sum = keep + swap_core(send)
    chip_sum, first_two, second_two = lax.optimization_barrier((chip_sum, first_two, second_two))
    share = chip_sum + swap_far(chip_sum)
    halves = s.reshape(2, 2, 4, XT * ROWS, LANES)
    stiff_two = jnp.where(core == 0, halves[:, 0], halves[:, 1])
    first_new = first_two + (1.0 - BETA_ONE) * share
    second_new = second_two + (1.0 - BETA_TWO) * share * share
    updated = stiff_two - LEARN_RATE * (first_new / (1.0 - BETA_ONE**ADAM_TICKS)) / (
        jnp.sqrt(second_new / (1.0 - BETA_TWO**ADAM_TICKS)) + ADAM_EPS
    )
    stiffness_new = finish(updated, swap_core(updated))
    first_new = jnp.where(far == 0, first_new[0], first_new[1])
    second_new = jnp.where(far == 0, second_new[0], second_new[1])
    return (from_native(stiffness_new), from_native(first_new), from_native(second_new))


def solution(mesh):
    return jax.shard_map(
        body,
        mesh=mesh,
        in_specs=(
            P(None, "gy", None),
            P("shot", "gy", None),
            P("shot", "gy", None),
            P("shot", None, "gy", None),
            P("shot", None, "gy", None),
            P("shot", None, "gy", None),
            P("shot", None, "gy", None),
            P("shot", None, "gy", None),
            P("shot", "gy", None),
            P("shot", None),
            P("shot", None),
        ),
        out_specs=(P(None, "gy", None), P("shot", "gy", None), P("shot", "gy", None)),
        check_vma=False,
    )
```

```python
import functools

import jax
import jax.numpy as jnp
from jax import lax
from jax.experimental import pallas as pl
from jax.experimental.pallas import tpu as pltpu
from jax.sharding import PartitionSpec as P

TIME_STEP_SQ = 0.15
BETA_ONE = 0.9
BETA_TWO = 0.999
LEARN_RATE = 0.05
ADAM_EPS = 1e-08
ADAM_TICKS = 10.0

NZ = 16
ROWS = 8
XT = 8
LANES = 128
STEPS = 4
REACH = STEPS + 1
EDGE = STEPS
CONE = STEPS - 1
OFF = ROWS
EXT = ROWS + 2 * OFF
FIELD = (EXT, NZ, XT, LANES)
SHORT = (ROWS + 2 * REACH, NZ, XT, LANES)
SURF_ROWS = ROWS + 2 * EDGE
PART = NZ // 2
TIP = CONE * (CONE + 1) // 2
TILE_S = REACH * PART + TIP
TILE_U = (2 * REACH - 1) * NZ + 2 * TIP + 2
TILE_A = TILE_S + TILE_U
TILE_L = (2 * REACH - 1) * NZ
HALF = 0.5 * TIME_STEP_SQ
PACK_VMEM = 56 << 20
FIRST_VMEM = 119 << 19

f32 = jnp.float32
VMEM = pl.BlockSpec(memory_space=pltpu.VMEM)
SMEM = pl.BlockSpec(memory_space=pltpu.SMEM)


def native(block):
    planes = block.shape[0]
    return block.reshape(planes, ROWS, XT, LANES).transpose(0, 2, 1, 3).reshape(planes, XT * ROWS, LANES)


def from_native(block):
    planes = block.shape[0]
    return block.reshape(planes, XT, ROWS, LANES).transpose(0, 2, 1, 3).reshape(planes, ROWS, XT * LANES)


def row_of(ref, z, y):
    return ref[z, pl.ds(y, XT, stride=ROWS), :]


def x_next(f, lane):
    r = pltpu.roll(f, LANES - 1, 1)
    return jnp.where(lane == LANES - 1, pltpu.roll(r, XT - 1, 0), r)


def x_prev(f, lane):
    r = pltpu.roll(f, 1, 1)
    return jnp.where(lane == 0, pltpu.roll(r, 1, 0), r)


def iotas():
    lane = lax.broadcasted_iota(jnp.int32, (XT, LANES), 1)
    tile = lax.broadcasted_iota(jnp.int32, (XT, LANES), 0)
    return lane, tile


def in_blocks(lo, hi, size, rows):
    whole = (hi - lo) // size
    if whole:
        lax.fori_loop(0, whole, lambda i, c: (rows(lo + i * size, size), c)[1], 0)
    if (hi - lo) % size:
        rows(lo + whole * size, (hi - lo) % size)


def pack_fields(fields, widths, low, high, at):
    def plane(z, carry):
        first = at
        for ref, width in zip(fields, widths, strict=True):
            for k in range(width):
                low[first + k * NZ + z] = row_of(ref, z, k)
                high[first + k * NZ + z] = row_of(ref, z, ROWS - width + k)
            first += width * NZ
        return carry

    lax.fori_loop(0, NZ, plane, 0)
    return at + sum(widths) * NZ


def core_index():
    return lax.rem(lax.axis_index("shot"), 2)


def by_parity(pair, work):
    parity = lax.rem(lax.axis_index("gy"), 2)

    @pl.when(parity == 0)
    def _():
        work(pair[1], pair[0])

    @pl.when(parity == 1)
    def _():
        work(pair[0], pair[1])


def pack_cone(ref, width, low, high, at):
    for k in range(CONE):
        for z in range(CONE - k):
            low[at] = row_of(ref, z, width + k)
            high[at] = row_of(ref, z, ROWS - 1 - width - k)
            at += 1
    return at


def fetch(sources, places, sems):
    copies = [pltpu.make_async_copy(a, b, sems.at[i]) for i, (a, b) in enumerate(zip(sources, places, strict=True))]
    for copy in copies:
        copy.start()
    for copy in copies:
        copy.wait()


def pack_first_kernel(
    s_far, u1_far, u0_far, receivers_far, observed_far, even, odd, s, u1, u0, receivers, observed, sems
):
    fetch((s_far, u1_far, u0_far, receivers_far, observed_far), (s, u1, u0, receivers, observed), sems)
    base = core_index() * PART

    def work(low, high):
        def plane(z, carry):
            for k in range(REACH):
                low[k * PART + z] = row_of(s, base + z, k)
                high[k * PART + z] = row_of(s, base + z, ROWS - REACH + k)
            return carry

        lax.fori_loop(0, PART, plane, 0)
        at = pack_cone(s, REACH, low, high, REACH * PART)
        at = pack_fields((u1, u0), (REACH, REACH - 1), low, high, at)
        at = pack_cone(u1, REACH, low, high, at)
        at = pack_cone(u0, REACH - 1, low, high, at)
        where = receivers[...].astype(f32)
        empty = jnp.zeros((2, LANES), f32)
        for side, rows in ((low, lambda n: slice(0, n)), (high, lambda n: slice(ROWS - n, ROWS))):
            parts = [where[rows(EDGE)]]
            for k in range(STEPS - 1, -1, -1):
                parts.append(observed[k][rows(k + 1)])
            parts.append(empty)
            both = jnp.concatenate(parts, 0)
            side[at] = both[:XT]
            side[at + 1] = both[XT:]

    by_parity((even, odd), work)


def pack_adjoint_kernel(l6_far, l7_far, even, odd, l6, l7, sems):
    fetch((l6_far, l7_far), (l6, l7), sems)
    by_parity((even, odd), lambda low, high: pack_fields((l6, l7), (REACH, REACH - 1), low, high, 0))


def pack(kernel, name, tiles, kept, limit, *arrays):
    shape = pltpu.VMEM((tiles, XT, LANES), f32)
    here = [pltpu.VMEM(a.shape, a.dtype) for a in arrays]
    return pl.pallas_call(
        kernel,
        out_shape=(shape, shape, *here[:kept]),
        in_specs=[pl.BlockSpec(memory_space=pl.ANY)] * len(arrays),
        out_specs=(VMEM,) * (2 + kept),
        scratch_shapes=here[kept:] + [pltpu.SemaphoreType.DMA((len(arrays),))],
        compiler_params=pltpu.CompilerParams(vmem_limit_bytes=limit),
        cost_estimate=pl.CostEstimate(flops=0, bytes_accessed=1 << 16, transcendentals=0),
        name=name,
    )(*arrays)


def fill(ext, own, off):
    def plane(z, carry):
        for k in range(ROWS):
            ext[off + k, z] = row_of(own, z, k)
        return carry

    lax.fori_loop(0, NZ, plane, 0)


def fill_halo(ext, off, low, high, at, width):
    for k in range(width):
        ext[off - width + k] = low[at + k * NZ : at + (k + 1) * NZ]
        ext[off + ROWS + k] = high[at + k * NZ : at + (k + 1) * NZ]


def fill_cone(ext, low, high, at, width):
    for k in range(CONE):
        planes = CONE - k
        ext[OFF - 1 - width - k, :planes] = low[at : at + planes]
        ext[OFF + ROWS + width + k, :planes] = high[at : at + planes]
        at += planes


def coefficients(stiff, diag, cx, cy, cz, lane, tile):
    x_end = (lane == LANES - 1) & (tile == XT - 1)
    x_start = (lane == 0) & (tile == 0)
    top, bottom = OFF - REACH, OFF + ROWS + REACH

    def face_y(e, planes):
        for z in range(planes):
            cy[e, z] = HALF * (stiff[e, z] + stiff[e + 1, z])

    def cells(e, planes):
        below = None
        following = HALF * stiff[e, 0]
        for z in range(planes):
            s = following
            face = s + jnp.where(x_end, 0.0, x_next(s, lane))
            total = face + (s + jnp.where(x_start, 0.0, x_prev(s, lane)))
            if z < NZ - 1:
                following = HALF * stiff[e, z + 1]
                above = s + following
            else:
                above = s
            total = total + above + (below if z > 0 else s) + cy[e, z] + cy[e - 1, z]
            cx[e, z] = jnp.where(x_end, 0.0, face)
            cz[e, z] = above
            diag[e, z] = 2.0 - total
            below = above

    def faces(first, count):
        for r in range(count):
            face_y(first + r, NZ)

    def rows(first, count):
        for r in range(count):
            cells(first + r, NZ)

    in_blocks(top, bottom - 1, 4, faces)
    for k in range(CONE):
        face_y(top - 1 - k, CONE - k)
        face_y(bottom - 1 + k, CONE - k)
    in_blocks(top + 1, bottom - 1, 4, rows)
    for k in range(CONE):
        cells(top - k, CONE - k)
        cells(bottom - 1 + k, CONE - k)


def leap(now, before, after, base, diag, cx, cy, cz, rows, lane, slope, inject=None):
    for e, planes in rows:
        f = e - base
        for z in range(planes):
            u = now[f, z]
            c = cx[e, z]
            following = x_next(u, lane)
            acc = diag[e, z] * u - before[f, z]
            acc = acc + c * following + x_prev(c * u, lane)
            acc = acc + cy[e, z] * now[f + 1, z] + cy[e - 1, z] * now[f - 1, z]
            if z < NZ - 1:
                acc = acc + cz[e, z] * now[f, z + 1]
            if z > 0:
                acc = acc + cz[e, z - 1] * now[f, z - 1]
            if z == 0 and inject is not None:
                acc = acc + inject[e - OFF + EDGE]
            after[f, z] = acc
            if OFF <= e < OFF + ROWS:
                slope[e - OFF, z] = following - u


def inner_rows(k):
    return [(OFF + y, NZ) for y in range(k + 1, ROWS - 1 - k)]


def step_rows(k, cone, skip=()):
    whole = STEPS - k
    rows = [(OFF + y, NZ) for y in range(ROWS)]
    rows += [(OFF - whole + j, NZ) for j in range(whole)] + [(OFF + ROWS + j, NZ) for j in range(whole)]
    if cone:
        for j in range(CONE):
            planes = min(CONE - j, whole)
            rows += [(OFF - 1 - whole - j, planes), (OFF + ROWS + whole + j, planes)]
    return [row for row in rows if row not in skip]


def three_parts(f):
    parts = []
    for _ in range(3):
        part = f.astype(jnp.bfloat16)
        parts.append(part.astype(f32))
        f = f - parts[-1]
    return jnp.concatenate(parts, 0).astype(jnp.bfloat16)


def misfit_surfaces(waves, receivers, observed, edges, surf, lane, tile):
    column = lax.broadcasted_iota(jnp.int32, (LANES, LANES), 0)
    plan = []
    for j in range(SURF_ROWS):
        y = j - EDGE
        if y < 0:
            used, at = range(-y - 1, STEPS), edges[0][:EDGE].astype(jnp.int32)[j : j + 1]
        elif y < ROWS:
            used, at = range(STEPS), receivers[y : y + 1, :]
        else:
            used, at = range(y - ROWS, STEPS), edges[1][:EDGE].astype(jnp.int32)[y - ROWS : y - ROWS + 1]
        pick = jnp.where(column == (at & (LANES - 1)), 1.0, 0.0).astype(jnp.bfloat16)
        held = jnp.where(tile == (at >> 7), 1.0, 0.0)
        surface = jnp.concatenate([waves[k + 1][OFF + y, 0] for k in used], 0)
        lanes_of = jnp.dot(three_parts(surface), pick, preferred_element_type=f32)
        plan.append((j, used, pick, held, lanes_of))
    for j, used, pick, held, lanes_of in plan:
        y = j - EDGE
        size = len(used) * XT
        lanes_of = lanes_of[:size] + lanes_of[size : 2 * size] + lanes_of[2 * size :]
        parts = []
        for i, k in enumerate(used):
            record = jnp.sum(lanes_of[i * XT : (i + 1) * XT] * held, axis=0, keepdims=True)
            if 0 <= y < ROWS:
                trace = observed[k, y : y + 1, :]
            else:
                skip = EDGE + sum(m + 1 for m in range(k + 1, STEPS))
                r = skip + (y + k + 1 if y < 0 else y - ROWS)
                trace = edges[0 if y < 0 else 1][r : r + 1]
            parts.append(held * (record - trace))
        back = lax.dot_general(
            three_parts(jnp.concatenate(parts, 0)), pick, (((1,), (1,)), ((), ())), preferred_element_type=f32
        )
        back = back[:size] + back[size : 2 * size] + back[2 * size :]
        for i, k in enumerate(used):
            surf[k, j] = back[i * XT : (i + 1) * XT]


def forward_kernel(
    source_pos, source_wave, u0, u1, s, even, odd, other, receivers, observed, l6, l7,
    w1, w2, w3, w4, w5, d1, d2, d3, d4, d5, diag, cx, cy, cz, surf, m6, m5, m4, m3, m_before, g6, g5, g4,
    stiff, before, edge,
):
    lane, tile = iotas()
    waves = (w1, w2, w3, w4, w5)
    slopes = (d1, d2, d3, d4)
    for ext, own in ((stiff, s), (w1, u1), (before, u0)):
        fill(ext, own, OFF)
    core = core_index()

    def halos(low, high):
        for part, base in ((0, core * PART), (1, (1 - core) * PART)):
            for k in range(REACH):
                stiff[OFF - REACH + k, pl.ds(base, PART)] = low[part][k * PART : (k + 1) * PART]
                stiff[OFF + ROWS + k, pl.ds(base, PART)] = high[part][k * PART : (k + 1) * PART]
        low, high = low[0], high[0]
        fill_cone(stiff, low, high, REACH * PART, REACH)
        at = TILE_S
        fill_halo(w1, OFF, low, high, at, REACH)
        at += REACH * NZ
        fill_halo(before, OFF, low, high, at, REACH - 1)
        at += (REACH - 1) * NZ
        fill_cone(w1, low, high, at, REACH)
        fill_cone(before, low, high, at + TIP, REACH - 1)
        for i, ref in enumerate((low, high)):
            edge[2 * i] = ref[TILE_A - 2]
            edge[2 * i + 1] = ref[TILE_A - 1]

    by_parity(((even, other.at[:TILE_S]), (odd, other.at[TILE_S:])), halos)
    coefficients(stiff, diag, cx, cy, cz, lane, tile)
    gy = lax.axis_index("gy")

    @pl.when(gy == 0)
    def _():
        cy[OFF - 1] = jnp.zeros((NZ, XT, LANES), f32)

    @pl.when(gy == lax.axis_size("gy") - 1)
    def _():
        cy[OFF + ROWS - 1] = jnp.zeros((NZ, XT, LANES), f32)

    z_src = source_pos[0, 0]
    e_src = source_pos[0, 1] - gy * ROWS + OFF
    x_src = source_pos[0, 2]
    spot = (tile * LANES + lane) == x_src
    for k in range(STEPS):
        older = before if k == 0 else waves[k - 1]
        after = waves[k + 1]
        leap(waves[k], older, after, 0, diag, cx, cy, cz, step_rows(k, True), lane, slopes[k])
        reach = STEPS - k + CONE

        @pl.when((e_src >= OFF - reach) & (e_src < OFF + ROWS + reach))
        def _():
            add = jnp.where(spot, TIME_STEP_SQ * source_wave[0, k], 0.0)
            after[e_src, z_src] = after[e_src, z_src] + add

    def last_slope(i, carry):
        for y in (4 * i + r for r in range(4)):
            for z in range(NZ):
                u = w5[OFF + y, z]
                d5[y, z] = x_next(u, lane) - u
        return carry

    lax.fori_loop(0, ROWS // 4, last_slope, 0)
    edges = [jnp.concatenate([edge[2 * i], edge[2 * i + 1]], 0) for i in range(2)]
    misfit_surfaces(waves, receivers, observed, edges, surf, lane, tile)

    fill(m6, l6, REACH)
    fill(m_before, l7, REACH)
    lams = (m6, m5, m4, m3)
    for k, slope in enumerate((g6, g5, g4)):
        older = m_before if k == 0 else lams[k - 1]
        leap(
            lams[k], older, lams[k + 1], OFF - REACH, diag, cx, cy, cz, inner_rows(k), lane, slope, surf.at[STEPS - 1 - k]
        )


def forward(*args):
    one = jax.ShapeDtypeStruct(FIELD, f32)
    own = jax.ShapeDtypeStruct((ROWS, NZ, XT, LANES), f32)
    surf = jax.ShapeDtypeStruct((STEPS, SURF_ROWS, XT, LANES), f32)
    short = jax.ShapeDtypeStruct(SHORT, f32)
    outs = (one,) * (STEPS + 1) + (own,) * (STEPS + 1) + (one,) * 4 + (surf,) + (short,) * 5 + (own,) * 3
    return pl.pallas_call(
        forward_kernel,
        out_shape=outs,
        in_specs=[SMEM] * 2 + [VMEM] * (len(args) - 2),
        out_specs=(VMEM,) * len(outs),
        scratch_shapes=[pltpu.VMEM(FIELD, f32)] * 2 + [pltpu.VMEM((4, XT, LANES), f32)],
        compiler_params=pltpu.CompilerParams(vmem_limit_bytes=16 << 20),
        cost_estimate=pl.CostEstimate(flops=1 << 25, bytes_accessed=1 << 24, transcendentals=0),
        name="forward",
    )(*args)


def adjoint_kernel(
    odd, even, w1, w2, w3, w4, w5, d1, d2, d3, d4, d5, diag, cx, cy, cz, surf, *rest
):
    m6, m5, m4, m3, before, g6, g5, g4, keep, send, m2, g3, face_y, grad = rest[8:]
    lane, tile = iotas()
    x_end = (lane == LANES - 1) & (tile == XT - 1)
    x_side = x_end | ((lane == 0) & (tile == 0))
    lams = (m6, m5, m4, m3, m2)
    slopes = (g6, g5, g4, g3)

    def halos(low, high):
        fill_halo(m6, REACH, low, high, 0, REACH)
        fill_halo(before, REACH, low, high, REACH * NZ, REACH - 1)

    by_parity((even, odd), halos)
    for k in range(STEPS):
        older = before if k == 0 else lams[k - 1]
        rows = step_rows(k, False, inner_rows(k))
        leap(lams[k], older, lams[k + 1], OFF - REACH, diag, cx, cy, cz, rows, lane, slopes[k], surf.at[STEPS - 1 - k])

    pairs = ((w5, m6, d5, g6), (w4, m5, d4, g5), (w3, m4, d3, g4), (w2, m3, d2, g3), (w1, m2, d1, None))
    for z in range(NZ):
        total = None
        for w, m, _, _ in pairs:
            part = (w[OFF, z] - w[OFF - 1, z]) * (m[REACH, z] - m[REACH - 1, z])
            total = part if total is None else total + part
        face_y[z] = total

    def two_rows(i, carry):
        below_y = [face_y[z] for z in range(NZ)]
        for y in (2 * i, 2 * i + 1):
            e = y + OFF
            below = None
            us = [w[e, 0] for w, _, _, _ in pairs]
            f = y + REACH
            ls = [m[f, 0] for _, m, _, _ in pairs]
            for z in range(NZ):
                fx = fy = fz = cell = None
                next_us, next_ls = [], []
                for (w, m, d, g), u, l in zip(pairs, us, ls, strict=True):
                    px = d[y, z] * (g[y, z] if g is not None else x_next(l, lane) - l)
                    py = (w[e + 1, z] - u) * (m[f + 1, z] - l)
                    both = u * l
                    if z < NZ - 1:
                        un, ln = w[e, z + 1], m[f, z + 1]
                        next_us.append(un)
                        next_ls.append(ln)
                        pz = (un - u) * (ln - l)
                    else:
                        pz = both
                    fx = px if fx is None else fx + px
                    fy = py if fy is None else fy + py
                    fz = pz if fz is None else fz + pz
                    cell = both if cell is None else cell + both
                us, ls = next_us, next_ls
                fx = jnp.where(x_end, 0.0, fx)
                total = fx + x_prev(fx, lane) + jnp.where(x_side, cell, 0.0)
                total = total + fy + below_y[z] + fz + (cell if z == 0 else below)
                below_y[z] = fy
                below = fz
                grad[z, pl.ds(y, XT, stride=ROWS), :] = -HALF * total
        for z in range(NZ):
            face_y[z] = below_y[z]
        return carry

    lax.fori_loop(0, ROWS // 2, two_rows, 0)
    core = core_index()
    for group in range(2):
        keep[group] = grad[pl.ds(8 * group + 4 * core, 4)]
        send[group] = grad[pl.ds(8 * group + 4 * (1 - core), 4)]


def adjoint(*args):
    part = jax.ShapeDtypeStruct((2, 4, XT * ROWS, LANES), f32)
    own = jax.ShapeDtypeStruct((ROWS, NZ, XT, LANES), f32)
    outs = (jax.ShapeDtypeStruct(SHORT, f32),) * 5 + (own,) * 3 + (part, part)
    first = len(args) - 8
    return pl.pallas_call(
        adjoint_kernel,
        out_shape=outs,
        in_specs=[VMEM] * len(args),
        out_specs=(VMEM,) * len(outs),
        input_output_aliases={first + i: i for i in range(8)},
        scratch_shapes=[
            pltpu.VMEM(SHORT, f32),
            pltpu.VMEM((ROWS, NZ, XT, LANES), f32),
            pltpu.VMEM((NZ, XT, LANES), f32),
            pltpu.VMEM((NZ, XT * ROWS, LANES), f32),
        ],
        compiler_params=pltpu.CompilerParams(vmem_limit_bytes=16 << 20),
        cost_estimate=pl.CostEstimate(flops=1 << 25, bytes_accessed=1 << 24, transcendentals=0),
        name="adjoint",
    )(*args)[-2:]


def blend_kernel(first, second, moments, first_two, second_two):
    far = lax.axis_index("shot") // 2
    first_two[far] = BETA_ONE * first[...]
    first_two[1 - far] = BETA_ONE * moments[0]
    second_two[far] = BETA_TWO * second[...]
    second_two[1 - far] = BETA_TWO * moments[1]


def blend(first, second, moments):
    two = jax.ShapeDtypeStruct((2, 4, XT * ROWS, LANES), f32)
    return pl.pallas_call(
        blend_kernel,
        out_shape=(two, two),
        in_specs=[VMEM] * 3,
        out_specs=(VMEM, VMEM),
        compiler_params=pltpu.CompilerParams(vmem_limit_bytes=4 << 20),
        cost_estimate=pl.CostEstimate(flops=0, bytes_accessed=1 << 24, transcendentals=0),
        name="blend",
    )(first, second, moments)


def finish_kernel(mine, other, out, sems):
    core = core_index()
    copies = []
    for group in range(2):
        for i, (part, base) in enumerate(((mine, core), (other, 1 - core))):
            target = out.at[pl.ds(8 * group + 4 * base, 4)]
            copies.append(pltpu.make_async_copy(part.at[group], target, sems.at[2 * group + i]))
    for copy in copies:
        copy.start()
    for copy in copies:
        copy.wait()


def finish(mine, other):
    return pl.pallas_call(
        finish_kernel,
        out_shape=jax.ShapeDtypeStruct((NZ, XT * ROWS, LANES), f32),
        in_specs=[VMEM, VMEM],
        out_specs=pl.BlockSpec(memory_space=pl.ANY),
        scratch_shapes=[pltpu.SemaphoreType.DMA((4,))],
        compiler_params=pltpu.CompilerParams(vmem_limit_bytes=2 << 20),
        name="finish",
    )(mine, other)


def swap_even(block):
    count = lax.axis_size("gy")
    pairs = [(i, i + 1) for i in range(0, count - 1, 2)]
    return lax.ppermute(block, "gy", pairs + [(j, i) for i, j in pairs])


def swap_odd(block):
    count = lax.axis_size("gy")
    pairs = [(i, i + 1) for i in range(1, count - 1, 2)]
    return lax.ppermute(block, "gy", pairs + [(j, i) for i, j in pairs])


def swap_core(block):
    return lax.ppermute(block, "shot", [(0, 1), (1, 0), (2, 3), (3, 2)])


def swap_far(block):
    return lax.ppermute(block, "shot", [(0, 2), (2, 0), (1, 3), (3, 1)])


def body(
    stiffness,
    first_moment,
    second_moment,
    wave_prev,
    wave_now,
    adjoint_next,
    adjoint_now,
    observed,
    receiver_x,
    source_pos,
    source_wave,
):
    shot = lax.axis_index("shot")
    core, far = shot % 2, shot // 2
    s = native(stiffness)
    u0, u1 = native(wave_prev[0]), native(wave_now[0])
    l6, l7 = native(adjoint_now[0]), native(adjoint_next[0])
    first, second = native(first_moment), native(second_moment)

    a_even, a_odd, s_here, u1, u0 = pack(
        pack_first_kernel, "pack_first", TILE_A, 3, FIRST_VMEM, s, u1, u0, receiver_x[0], observed[0])
    l_even, l_odd = pack(pack_adjoint_kernel, "pack_adjoint", TILE_L, 0, PACK_VMEM, l6, l7)
    a_even, a_odd = swap_even(a_even), swap_odd(a_odd)
    moments = jnp.stack([first, second])
    l_even, l_odd, moments, a_even = lax.optimization_barrier((l_even, l_odd, moments, a_even))
    l_even, l_odd, moments = swap_even(l_even), swap_odd(l_odd), swap_far(moments)
    other = swap_core(jnp.concatenate([a_even[:TILE_S], a_odd[:TILE_S]]))
    fields = forward(
        source_pos, source_wave, u0, u1, s_here, a_even, a_odd, other, receiver_x[0], observed[0], l6, l7
    )
    keep, send = adjoint(l_odd, l_even, *fields)
    keep, moments = lax.optimization_barrier((keep, moments))
    first_two, second_two = blend(first, second, moments)
    chip_sum = keep + swap_core(send)
    chip_sum, first_two, second_two = lax.optimization_barrier((chip_sum, first_two, second_two))
    share = chip_sum + swap_far(chip_sum)
    halves = s.reshape(2, 2, 4, XT * ROWS, LANES)
    stiff_two = jnp.where(core == 0, halves[:, 0], halves[:, 1])
    first_new = first_two + (1.0 - BETA_ONE) * share
    second_new = second_two + (1.0 - BETA_TWO) * share * share
    updated = stiff_two - LEARN_RATE * (first_new / (1.0 - BETA_ONE**ADAM_TICKS)) / (
        jnp.sqrt(second_new / (1.0 - BETA_TWO**ADAM_TICKS)) + ADAM_EPS
    )
    stiffness_new = finish(updated, swap_core(updated))
    first_new = jnp.where(far == 0, first_new[0], first_new[1])
    second_new = jnp.where(far == 0, second_new[0], second_new[1])
    return (from_native(stiffness_new), from_native(first_new), from_native(second_new))


def solution(mesh):
    return jax.shard_map(
        body,
        mesh=mesh,
        in_specs=(
            P(None, "gy", None),
            P("shot", "gy", None),
            P("shot", "gy", None),
            P("shot", None, "gy", None),
            P("shot", None, "gy", None),
            P("shot", None, "gy", None),
            P("shot", None, "gy", None),
            P("shot", None, "gy", None),
            P("shot", "gy", None),
            P("shot", None),
            P("shot", None),
        ),
        out_specs=(P(None, "gy", None), P("shot", "gy", None), P("shot", "gy", None)),
        check_vma=False,
    )
```
